128 devices in a mesh: view: 8 (over x, core), band: 16 (over y, z).
Axes of the slice: x: 4, y: 4, z: 4, core: 2. Of those that a mesh axis runs over, the one named last changes fastest.
Arguments:
- positions: float32 [3, 65536], P(None, 'band'), may hold values from -48 to 48
- log_scales: float32 [3, 65536], P(None, 'band'), may hold values from -0.7 to 0.7
- rotations: float32 [4, 65536], P(None, 'band'), may hold values from 0.3 to 1.5
- opacity_logit: float32 [1, 65536], P(None, 'band'), may hold values from -6 to -2
- sh_coeffs: float32 [48, 65536], P(None, 'band'), may hold values from -1.8 to 1.8
- view_angles: float32 [8, 2], P('view'), may hold values from -3.140625 to 3.140625
- target: float32 [8, 768, 3, 256], P('view', 'band'), may hold values from -2 to 3
- fetch_index: int32 [8, 16, 16, 512], P('view', 'band'), may hold values from 0 to 4095, as said below
- tile_slots: int32 [8, 768, 256], P('view', 'band'), may hold values from 0 to 8191, as said below
- depth_order: int32 [8, 768, 256], P('view', 'band'), may hold values from 0 to 255, each once within a row
- block_count: int32 [8, 768], P('view', 'band'), may hold values from 64 to 256, as said below
Outputs:
- images: float32 [8, 768, 3, 256], P('view', 'band')
- view_loss: float32 [8], P('view')
- grad_positions: float32 [3, 65536], P(None, 'band')
- grad_log_scales: float32 [3, 65536], P(None, 'band')
- grad_rotations: float32 [4, 65536], P(None, 'band')
- grad_opacity: float32 [1, 65536], P(None, 'band')
- grad_sh: float32 [48, 65536], P(None, 'band')
The draws below stay inside these ranges and needn't reach their ends.
Inputs may be any that keep to these rules, and one draw needn't show every extreme that they name: `fetch_index`: the 512 entries for one view, band and owner are distinct. `tile_slots`: entry o * 512 + c names the c-th Gaussian that the tile's band requests from owner o; in each view the last owner's request lists, and those of one owner drawn from the seed, are used in full by every band, the others' only in part. `block_count`: each band of each view has a tile with all 256 positions live.
All inputs are finite; a program needn't handle non-finite values.
Results may differ from the reference program's by a relative error of at most 0.0003.
Values sent between devices are 32-bit elements; how exact they have to be, the bound alone decides.
No kernel may reach another device: no remote copies, remote signals or barrier semaphores. Data moves between devices by JAX's collectives and lax.ppermute only.
A program may use at most 128 MiB of HBM per device.

```python
import math
from functools import partial
import jax
import jax.numpy as jnp
from jax import lax

TILE_SIDE = 16
SLOTS = 256
TILE_DEV = 48
CAP = 512
G_DEV = 4096
VIEWS = 8
BANDS = 16
TILES = 768
GAUSS = 65536


def draw_target(key, part):
    key = jax.random.fold_in(key, 5)
    shape = (VIEWS, TILES, 3, TILE_SIDE * TILE_SIDE)
    position = (jnp.arange(TILES, dtype=jnp.float32) / max(TILES - 1, 1)).reshape(1, TILES, 1, 1)
    spread = 0.25 * (1.0 + 2.0 * position)
    noise = jax.random.truncated_normal(key, -3.0, 3.0, shape, jnp.float32)
    return (0.5 + spread * noise).astype(jnp.float32)


def draw_fetch_index(key, part):
    key = jax.random.fold_in(key, 3)
    keys = jax.random.split(key, VIEWS * BANDS * BANDS)
    picks = jax.vmap(lambda single: jax.random.permutation(single, G_DEV)[:CAP])(keys)
    return picks.reshape(VIEWS, BANDS, BANDS, CAP).astype(jnp.int32)


def draw_tile_slots(key, part):
    key = jax.random.fold_in(key, 2)
    hot_key, rest_key, owner_key, column_key = jax.random.split(key, 4)
    hot = jax.random.randint(hot_key, (VIEWS, 1, 1), 0, BANDS)
    rest = jax.random.randint(rest_key, (VIEWS, BANDS, BANDS), CAP // 8, CAP // 2 + 1)
    owner_ids = jnp.arange(BANDS, dtype=jnp.int32).reshape(1, 1, BANDS)
    full_owner = (owner_ids == hot) | (owner_ids == BANDS - 1)
    counts = jnp.where(full_owner, CAP, rest)
    owner = jax.random.randint(owner_key, (VIEWS, TILES, SLOTS), 0, BANDS)
    raw = jax.random.randint(column_key, (VIEWS, TILES, SLOTS), 0, 1 << 20)
    band_of_tile = (jnp.arange(TILES, dtype=jnp.int32) // TILE_DEV).reshape(1, TILES, 1)
    view_ids = jnp.arange(VIEWS, dtype=jnp.int32).reshape(VIEWS, 1, 1)
    limit = counts[view_ids, band_of_tile, owner]
    slots = (owner * CAP + raw % limit).astype(jnp.int32)
    slots = slots.at[:, 0, 0].set(BANDS * CAP - 1)
    slots = slots.at[:, 0, 1].set(0)
    return slots.astype(jnp.int32)


def draw_block_count(key, part):
    key = jax.random.fold_in(key, 4)
    count_key, pick_key = jax.random.split(key)
    counts = jax.random.randint(count_key, (VIEWS, TILES), SLOTS // 4, SLOTS + 1)
    pick = jax.random.randint(pick_key, (VIEWS, BANDS, 1), 0, TILE_DEV)
    full = (jnp.arange(TILE_DEV, dtype=jnp.int32).reshape(1, 1, TILE_DEV) == pick).reshape(VIEWS, TILES)
    return jnp.where(full, SLOTS, counts).astype(jnp.int32)


def steps_of(key, dims, cuts, least, high):
    level = 1.0
    for axis_at, parts in cuts:
        steps = jax.random.uniform(jax.random.fold_in(jax.random.fold_in(key, 6), axis_at), (parts,), jnp.float32, least / len(cuts), high / len(cuts))
        level = level * jnp.repeat(jnp.exp(steps), dims[axis_at] // parts).reshape((-1,) + (1,) * (len(dims) - 1 - axis_at))
    return level


def bell_draw(rng, dims, scale, reach, pieces=(), kind=jnp.bfloat16):
    drawn = jax.random.normal(rng, dims, jnp.float32) * scale
    if len(pieces) > 0:
        drawn = steps_of(rng, dims, pieces, -0.22, 0.18) * drawn
    return jnp.clip(drawn, min=-reach, max=reach).astype(kind)


def setup_inputs(seed: int = 0) -> dict:
    arg_keys = jax.random.split(jax.random.key(seed), 12)
    return {
        "positions": bell_draw(arg_keys[0], (3, GAUSS), 8.0, 48.0, ((1, 16),), jnp.float32),
        "log_scales": jnp.clip(jax.random.uniform(arg_keys[1], (3, GAUSS), jnp.float32, -0.7, 0.7) * steps_of(arg_keys[1], (3, GAUSS), ((1, 16),), -0.4, 0.0), -0.7, 0.7),
        "rotations": jnp.clip(0.3 + 1.2 * jax.random.uniform(arg_keys[2], (4, GAUSS), jnp.float32) ** steps_of(arg_keys[2], (4, GAUSS), ((1, 16),), -0.2, 0.2), 0.3, 1.5),
        "opacity_logit": jnp.clip(-6.0 + 4.0 * jax.random.uniform(arg_keys[3], (1, GAUSS), jnp.float32) ** steps_of(arg_keys[3], (1, GAUSS), ((1, 16),), -0.2, 0.2), -6.0, -2.0),
        "sh_coeffs": bell_draw(arg_keys[4], (48, GAUSS), 0.3, 1.8, ((1, 16),), jnp.float32),
        "view_angles": jnp.clip(jax.random.uniform(arg_keys[5], (VIEWS, 2), jnp.float32, -3.140625, 3.140625), -3.140625, 3.140625),
        "target": draw_target(jax.random.fold_in(arg_keys[11], 71), 0),
        "fetch_index": draw_fetch_index(jax.random.fold_in(arg_keys[11], 71), 0),
        "tile_slots": draw_tile_slots(jax.random.fold_in(arg_keys[11], 71), 0),
        "depth_order": jax.vmap(lambda own: jax.random.permutation(own, SLOTS))(jax.random.split(arg_keys[9], VIEWS * TILES)).reshape((VIEWS, TILES, SLOTS)).astype(jnp.int32),
        "block_count": draw_block_count(jax.random.fold_in(arg_keys[11], 71), 0),
    }


zero_term = 0.28209479177387814
first_term = 0.4886025119029199
second_terms = (1.0925484305920792, -1.0925484305920792, 0.31539156525252005, -1.0925484305920792, 0.5462742152960396)
third_terms = (-0.5900435899266435, 2.890611442640554, -0.4570457994644658, 0.3731763325901154, -0.4570457994644658, 1.445305721320277, -0.5900435899266435)
dilation = 0.3
highest = lax.Precision.HIGHEST

def harmonic_basis(dir_x, dir_y, dir_z):
    square_x = dir_x * dir_x
    square_y = dir_y * dir_y
    square_z = dir_z * dir_z
    terms = [zero_term + 0.0 * dir_x, -first_term * dir_y, first_term * dir_z, -first_term * dir_x, second_terms[0] * dir_x * dir_y, second_terms[1] * dir_y * dir_z, second_terms[2] * (2.0 * square_z - square_x - square_y), second_terms[3] * dir_x * dir_z, second_terms[4] * (square_x - square_y), third_terms[0] * dir_y * (3.0 * square_x - square_y), third_terms[1] * dir_x * dir_y * dir_z, third_terms[2] * dir_y * (4.0 * square_z - square_x - square_y), third_terms[3] * dir_z * (2.0 * square_z - 3.0 * square_x - 3.0 * square_y), third_terms[4] * dir_x * (4.0 * square_z - square_x - square_y), third_terms[5] * dir_z * (square_x - square_y), third_terms[6] * dir_x * (square_x - 3.0 * square_y)]
    return jnp.stack(terms)

def project(angles, positions, log_scales, rotations, opacity_logit, sh_coeffs):
    cos_a, sin_a = (jnp.cos(angles[0]), jnp.sin(angles[0]))
    cos_e, sin_e = (jnp.cos(angles[1]), jnp.sin(angles[1]))
    right = (-sin_a, cos_a, 0.0 * sin_a)
    upward = (-sin_e * cos_a, -sin_e * sin_a, cos_e)
    mean_x = right[0] * positions[0] + right[1] * positions[1] + right[2] * positions[2]
    mean_y = upward[0] * positions[0] + upward[1] * positions[1] + upward[2] * positions[2]
    length = jnp.sqrt(lax.optimization_barrier(jnp.sum(rotations * rotations, axis=0)))
    quat_w = rotations[0] / length
    quat_x = rotations[1] / length
    quat_y = rotations[2] / length
    quat_z = rotations[3] / length
    matrix = [[1.0 - 2.0 * (quat_y * quat_y + quat_z * quat_z), 2.0 * (quat_x * quat_y - quat_w * quat_z), 2.0 * (quat_x * quat_z + quat_w * quat_y)], [2.0 * (quat_x * quat_y + quat_w * quat_z), 1.0 - 2.0 * (quat_x * quat_x + quat_z * quat_z), 2.0 * (quat_y * quat_z - quat_w * quat_x)], [2.0 * (quat_x * quat_z - quat_w * quat_y), 2.0 * (quat_y * quat_z + quat_w * quat_x), 1.0 - 2.0 * (quat_x * quat_x + quat_y * quat_y)]]
    scales = jnp.exp(log_scales)

    def screen_row(axis_row):
        return [(axis_row[0] * matrix[0][col] + axis_row[1] * matrix[1][col] + axis_row[2] * matrix[2][col]) * scales[col] for col in range(3)]
    first = screen_row(right)
    second = screen_row(upward)
    cov_a = first[0] * first[0] + first[1] * first[1] + first[2] * first[2] + dilation
    cov_b = first[0] * second[0] + first[1] * second[1] + first[2] * second[2]
    cov_c = second[0] * second[0] + second[1] * second[1] + second[2] * second[2] + dilation
    determinant = cov_a * cov_c - cov_b * cov_b
    opacity = jax.nn.sigmoid(opacity_logit[0])
    basis = harmonic_basis(cos_e * cos_a, cos_e * sin_a, sin_e)
    shaped = sh_coeffs.reshape((16, 3, sh_coeffs.shape[1]))
    colours = jnp.maximum(0.5 + lax.optimization_barrier(jnp.sum(basis[:, None, None] * shaped, axis=0)), 0.0)
    front = jnp.stack([mean_x, mean_y, cov_c / determinant, -cov_b / determinant, cov_a / determinant, opacity])
    return jnp.concatenate([front, colours], axis=0)

def blend_tile(compact, limit, goal):
    side = TILE_SIDE
    slot_total = compact.shape[1]
    pixel_ids = jnp.arange(side * side, dtype=jnp.int32)
    pixel_x = (pixel_ids % side).astype(jnp.float32) + 0.5
    pixel_y = (pixel_ids // side).astype(jnp.float32) + 0.5
    turn = 2.0 * math.pi / side
    delta_x = jnp.sin(turn * (pixel_x[:, None] - compact[0][None, :])) / turn
    delta_y = jnp.sin(turn * (pixel_y[:, None] - compact[1][None, :])) / turn
    power = compact[2][None, :] * delta_x * delta_x + 2.0 * compact[3][None, :] * delta_x * delta_y + compact[4][None, :] * delta_y * delta_y
    slot_ids = jnp.arange(slot_total, dtype=jnp.int32)
    live = (slot_ids < limit).astype(jnp.float32)
    alpha = (live * compact[5])[None, :] * jnp.exp(-0.5 * power)
    log_keep = jnp.log1p(-alpha)
    strict_upper = (slot_ids[:, None] < slot_ids[None, :]).astype(jnp.float32)
    depth = jnp.dot(log_keep, strict_upper, precision=highest, preferred_element_type=jnp.float32)
    weights = alpha * jnp.exp(depth)
    image = lax.dot_general(compact[6:9], weights, (((1,), (1,)), ((), ())), precision=highest, preferred_element_type=jnp.float32)
    error = image - goal
    return (0.5 * jnp.sum(error * error), image)

def tile_terms(compact, limit, goal):
    (value, image), grad = jax.value_and_grad(blend_tile, has_aux=True)(compact, limit, goal)
    return (value, image, grad)

def reference(positions, log_scales, rotations, opacity_logit, sh_coeffs, view_angles, target, fetch_index, tile_slots, depth_order, block_count):
    params = (positions, log_scales, rotations, opacity_logit, sh_coeffs)
    totals = [jnp.zeros_like(array) for array in params]
    tile_band = jnp.arange(TILES, dtype=jnp.int32) // TILE_DEV
    images = []
    losses = []
    for view in range(VIEWS):
        compact, pull = jax.vjp(partial(project, view_angles[view]), *params)
        ordered = jnp.take_along_axis(tile_slots[view], depth_order[view], axis=1)
        owner = ordered // CAP
        column = ordered % CAP
        local = fetch_index[view][tile_band[:, None], owner, column]
        global_ids = (owner * G_DEV + local).astype(jnp.int32)

        def one_tile(item):
            ids, limit, goal = item
            return tile_terms(compact[:, ids], limit, goal)
        values, pictures, grads = lax.map(one_tile, (global_ids, block_count[view], target[view]))
        flat_grads = jnp.transpose(grads, (1, 0, 2)).reshape(compact.shape[0], -1)
        cotangent = jnp.zeros_like(compact).at[:, global_ids.reshape(-1)].add(flat_grads)
        pulled = pull(cotangent)
        totals = [before + extra for before, extra in zip(totals, pulled)]
        images.append(pictures)
        losses.append(2.0 * jnp.sum(values) / (TILES * TILE_SIDE * TILE_SIDE * 3))
    return (jnp.stack(images), jnp.stack(losses), totals[0], totals[1], totals[2], totals[3], totals[4])
```

```python
import math

import jax
import jax.numpy as jnp
import ml_dtypes
import numpy as np
from jax import lax
from jax.experimental import pallas as pl
from jax.experimental.pallas import tpu as pltpu
from jax.sharding import PartitionSpec as P

SIDE = 16
PIX = SIDE * SIDE
SLOTS = 256
TILES = 48
CAP = 512
OWNERS = 16
LOCAL = 4096
VIEWS = 8
GROUP = 8
GROUPS = TILES // GROUP
ROWS = GROUP * SLOTS
CHUNK = 256
CHUNK_K = CHUNK // GROUP
CHUNKS = ROWS // CHUNK
SCAT = 512
TURN = 2.0 * math.pi / SIDE
KAPPA = 0.5 / (TURN * TURN)
LOG2E = 1.4426950408889634
DEAD = -1024.0
SEND_ROWS = 48
BACK_ROWS = 56
WIDE = LOCAL + 512 + 128

f32 = jnp.float32
bf16 = jnp.bfloat16

zero_term = 0.28209479177387814
first_term = 0.4886025119029199
second_terms = (
    1.0925484305920792,
    -1.0925484305920792,
    0.31539156525252005,
    -1.0925484305920792,
    0.5462742152960396,
)
third_terms = (
    -0.5900435899266435,
    2.890611442640554,
    -0.4570457994644658,
    0.3731763325901154,
    -0.4570457994644658,
    1.445305721320277,
    -0.5900435899266435,
)
dilation = 0.3


def pixel_tables():
    pixel = np.arange(PIX)
    ang_x = TURN * (pixel % SIDE + 0.5)
    ang_y = TURN * (pixel // SIDE + 0.5)
    sx, cx, sy, cy = np.sin(ang_x), np.cos(ang_x), np.sin(ang_y), np.cos(ang_y)
    rows = np.stack(
        [
            np.ones(PIX),
            np.cos(2 * ang_x),
            np.sin(2 * ang_x),
            np.cos(2 * ang_y),
            np.sin(2 * ang_y),
            sx * sy,
            sx * cy,
            cx * sy,
            cx * cy,
        ]
    )
    kind = ml_dtypes.bfloat16
    parts = []
    rest = rows
    for _ in range(3):
        part = rest.astype(kind)
        parts.append(part)
        rest = rest - part.astype(np.float64)
    order = (0, 1, 2, 0, 1, 0)
    front = np.zeros((128, PIX), kind)
    for at, which in enumerate(order):
        front[8 * at : 8 * at + 8] = parts[which][:8]
        front[48 + at] = parts[which][8]
    back = np.zeros((32, PIX), kind)
    back[0:9] = parts[0]
    back[16:25] = parts[1]
    return front, back


def harmonic_basis(dir_x, dir_y, dir_z):
    square_x = dir_x * dir_x
    square_y = dir_y * dir_y
    square_z = dir_z * dir_z
    return [
        zero_term + 0.0 * dir_x,
        -first_term * dir_y,
        first_term * dir_z,
        -first_term * dir_x,
        second_terms[0] * dir_x * dir_y,
        second_terms[1] * dir_y * dir_z,
        second_terms[2] * (2.0 * square_z - square_x - square_y),
        second_terms[3] * dir_x * dir_z,
        second_terms[4] * (square_x - square_y),
        third_terms[0] * dir_y * (3.0 * square_x - square_y),
        third_terms[1] * dir_x * dir_y * dir_z,
        third_terms[2] * dir_y * (4.0 * square_z - square_x - square_y),
        third_terms[3] * dir_z * (2.0 * square_z - 3.0 * square_x - 3.0 * square_y),
        third_terms[4] * dir_x * (4.0 * square_z - square_x - square_y),
        third_terms[5] * dir_z * (square_x - square_y),
        third_terms[6] * dir_x * (square_x - 3.0 * square_y),
    ]


def iota(shape, axis):
    return lax.broadcasted_iota(jnp.int32, shape, axis)


def wave(mean):
    cycles = mean * (1.0 / SIDE)
    part = cycles - jnp.floor(cycles + 0.5)
    x = part * math.pi
    x2 = x * x
    sine = 1.0 / 6227020800.0
    for scale in (-1.0 / 39916800.0, 1.0 / 362880.0, -1.0 / 5040.0, 1.0 / 120.0, -1.0 / 6.0, 1.0):
        sine = sine * x2 + scale
    sine = sine * x
    cosine = -1.0 / 87178291200.0
    for scale in (
        1.0 / 479001600.0,
        -1.0 / 3628800.0,
        1.0 / 40320.0,
        -1.0 / 720.0,
        1.0 / 24.0,
        -0.5,
        1.0,
    ):
        cosine = cosine * x2 + scale
    return 2.0 * sine * cosine, 1.0 - 2.0 * sine * sine


def rotation(rows):
    length = jnp.sqrt(
        rows[0] * rows[0] + rows[1] * rows[1] + rows[2] * rows[2] + rows[3] * rows[3]
    )
    inverse = 1.0 / length
    w, x, y, z = [row * inverse for row in rows]
    matrix = [
        [1.0 - 2.0 * (y * y + z * z), 2.0 * (x * y - w * z), 2.0 * (x * z + w * y)],
        [2.0 * (x * y + w * z), 1.0 - 2.0 * (x * x + z * z), 2.0 * (y * z - w * x)],
        [2.0 * (x * z - w * y), 2.0 * (y * z + w * x), 1.0 - 2.0 * (x * x + y * y)],
    ]
    return inverse, (w, x, y, z), matrix


def halves(value):
    high = value.astype(bf16)
    low = (value - high.astype(f32)).astype(bf16)
    return high, low


def pick(table, lanes):
    return jnp.take_along_axis(table, lanes, axis=1)


def project_kernel(cam, wanted, positions, log_scales, rotations, logit, sh, send, aux, tab):
    cos_a, sin_a, cos_e, sin_e = cam[0, 0], cam[0, 1], cam[0, 2], cam[0, 3]
    right = (-sin_a, cos_a)
    upward = (-sin_e * cos_a, -sin_e * sin_a, cos_e)
    basis = harmonic_basis(cos_e * cos_a, cos_e * sin_a, sin_e)
    pos = [positions[i : i + 1, :] for i in range(3)]
    mean_x = right[0] * pos[0] + right[1] * pos[1]
    mean_y = upward[0] * pos[0] + upward[1] * pos[1] + upward[2] * pos[2]
    _, _, matrix = rotation([rotations[i : i + 1, :] for i in range(4)])
    scales = [jnp.exp(log_scales[i : i + 1, :]) for i in range(3)]
    first = [(right[0] * matrix[0][j] + right[1] * matrix[1][j]) * scales[j] for j in range(3)]
    second = [
        (upward[0] * matrix[0][j] + upward[1] * matrix[1][j] + upward[2] * matrix[2][j])
        * scales[j]
        for j in range(3)
    ]
    cov_a = first[0] * first[0] + first[1] * first[1] + first[2] * first[2] + dilation
    cov_b = first[0] * second[0] + first[1] * second[1] + first[2] * second[2]
    cov_c = second[0] * second[0] + second[1] * second[1] + second[2] * second[2] + dilation
    inverse = 1.0 / (cov_a * cov_c - cov_b * cov_b)
    c0, c1, c2 = cov_c * inverse, -cov_b * inverse, cov_a * inverse
    sa, ca = wave(mean_x)
    sb, cb = wave(mean_y)
    unit = KAPPA * LOG2E
    g0 = -LOG2E * jnp.log(1.0 + jnp.exp(-logit[...])) - (0.5 * unit) * (c0 + c2)
    cross = (-2.0 * unit) * c1
    half_x, half_y = (0.5 * unit) * c0, (0.5 * unit) * c2
    features = [
        g0,
        half_x * (1.0 - 2.0 * sa * sa),
        half_x * (2.0 * sa * ca),
        half_y * (1.0 - 2.0 * sb * sb),
        half_y * (2.0 * sb * cb),
        cross * ca * cb,
        -cross * ca * sb,
        -cross * sa * cb,
        cross * sa * sb,
    ]
    row48 = iota((48, 128), 0)
    weight = jnp.zeros((48, 128), f32)
    for k in range(16):
        weight = jnp.where(row48 // 3 == k, basis[k], weight)
    residue = row48 % 3
    masks = [jnp.where(residue == c, weight, 0.0) for c in range(3)]
    for block in range(LOCAL // 128):
        lanes = slice(128 * block, 128 * block + 128)
        piece = sh[:, lanes]
        for c in range(3):
            raw = 0.5 + jnp.sum(masks[c] * piece, axis=0, keepdims=True)
            aux[7 + c : 8 + c, lanes] = raw
            tab[9 + c : 10 + c, lanes] = jnp.maximum(raw, 0.0)
    for at, row in enumerate(features):
        tab[at : at + 1, :] = row
    for at, row in enumerate((ca, sa, cb, sb, c0, c1, c2)):
        aux[at : at + 1, 0:LOCAL] = row
    aux[10:16, 0:LOCAL] = jnp.zeros((6, LOCAL), f32)
    lane = iota((8, 128), 1)
    sub = iota((8, 128), 0)
    coef = jnp.zeros((8, 128), f32)
    for k in range(16):
        coef = jnp.where((lane // 3 == k) & (sub == 5 + lane % 3), basis[k], coef)

    def put(base, row, at, value):
        return jnp.where((sub == row) & (lane == at), value, base)

    for i in range(3):
        if i < 2:
            coef = put(coef, 0, 48 + i, right[i])
        coef = put(coef, 1, 48 + i, upward[i])
    at = 51
    for i in range(3):
        for j in range(i, 3):
            if j < 2:
                coef = put(coef, 2, at, 2.0 * right[i] * right[j])
            mixed = 0.0
            if i < 2:
                mixed = mixed + right[i] * upward[j]
            if j < 2:
                mixed = mixed + right[j] * upward[i]
            if i < 2 or j < 2:
                coef = put(coef, 3, at, 2.0 * mixed)
            coef = put(coef, 4, at, 2.0 * upward[i] * upward[j])
            at += 1
    aux[0:8, LOCAL : LOCAL + 128] = coef
    aux[8:16, LOCAL : LOCAL + 128] = jnp.zeros((8, 128), f32)

    upper = sub >= 4

    def gather_band(band, carry):
        ids = [jnp.broadcast_to(wanted[band, j : j + 1, :], (8, 128)) for j in range(4)]
        spots = [value & 127 for value in ids]
        blocks = [lax.shift_right_logical(value, 7) for value in ids]
        acc = [jnp.zeros((8, 128), f32)] * 4
        low = [jnp.zeros((8, 128), f32)] * 4
        for block in range(LOCAL // 128):
            front = tab[0:8, 128 * block : 128 * block + 128]
            for j in range(4):
                acc[j] = jnp.where(blocks[j] == block, pick(front, spots[j]), acc[j])
        for pair in range(LOCAL // 256):
            first_half = tab[8:12, 256 * pair : 256 * pair + 128]
            second_half = tab[8:12, 256 * pair + 128 : 256 * pair + 256]
            both = jnp.concatenate([first_half, second_half], axis=0)
            which = jnp.where(upper, 2 * pair + 1, 2 * pair)
            for j in range(4):
                low[j] = jnp.where(blocks[j] == which, pick(both, spots[j]), low[j])
        for j in range(4):
            send[band, 8 * j : 8 * j + 8, :] = acc[j]
            whole = low[j] + pltpu.roll(low[j], 4, 0)
            send[band, 32 + 4 * j : 36 + 4 * j, :] = whole[0:4]
        return carry

    lax.fori_loop(0, OWNERS, gather_band, 0)


def blend_kernel(
    table,
    slots,
    order,
    counts,
    target,
    front,
    back,
    images,
    answer,
    lhs,
    colours,
    alpha_ref,
    weight_ref,
    high_ref,
    low_ref,
    ids_ref,
    grads,
    total,
):
    lane = iota((8, 128), 1)
    sub = iota((8, 128), 0)
    upper = sub >= 4
    diagonal = sub == (lane & 7)
    diag_wide = iota((8, CHUNK), 0) == (iota((8, CHUNK), 1) & 7)
    total[...] = jnp.zeros_like(total)

    def one_group(group, loss):
        start = pl.multiple_of(group * GROUP, GROUP)
        limit = jnp.broadcast_to(counts[pl.ds(group, 1), :], (8, 128))
        own = slots[pl.ds(start, GROUP), :]
        sequence = order[pl.ds(start, GROUP), :]
        ordered = []
        for half in range(2):
            seq = sequence[:, 128 * half : 128 * half + 128]
            spot = seq & 127
            ordered.append(
                jnp.where(seq < 128, pick(own[:, 0:128], spot), pick(own[:, 128:256], spot))
            )
        for half in range(2):

            def gather_part(part, carry, half=half):
                spots, blocks = [], []
                for j in range(4):
                    base = (part * 4 + j) * 16
                    value = pick(ordered[half], base + lax.shift_right_logical(lane, 3))
                    value = jnp.sum(jnp.where(diagonal, value, 0), axis=0, keepdims=True)
                    value = jnp.broadcast_to(value, (8, 128))
                    at = pl.multiple_of((half * 8 + part * 4 + j) * 128, 128)
                    ids_ref[:, pl.ds(at, 128)] = value
                    spots.append(value & 127)
                    blocks.append(lax.shift_right_logical(value, 7))
                acc = [jnp.zeros((8, 128), f32)] * 4
                low = [jnp.zeros((8, 128), f32)] * 4
                for block in range(64):
                    rows = table[block // 4, 8 * (block % 4) : 8 * (block % 4) + 8, :]
                    for j in range(4):
                        acc[j] = jnp.where(blocks[j] == block, pick(rows, spots[j]), acc[j])
                for pair in range(32):
                    rows = table[pair // 2, 32 + 8 * (pair % 2) : 40 + 8 * (pair % 2), :]
                    which = jnp.where(upper, 2 * pair + 1, 2 * pair)
                    for j in range(4):
                        low[j] = jnp.where(blocks[j] == which, pick(rows, spots[j]), low[j])
                for j in range(4):
                    at = pl.multiple_of((half * 8 + part * 4 + j) * 128, 128)
                    position = (half * 8 + part * 4 + j) * 16 + lax.shift_right_logical(lane, 3)
                    dead = position >= limit
                    value = jnp.where(dead & (sub == 0), DEAD, acc[j])
                    rest = low[j] + pltpu.roll(low[j], 4, 0)
                    p1 = value.astype(bf16).astype(f32)
                    p2 = (value - p1).astype(bf16).astype(f32)
                    p3 = value - p1 - p2
                    last = jnp.broadcast_to(rest[0:1], (8, 128))
                    q1 = last.astype(bf16).astype(f32)
                    q2 = (last - q1).astype(bf16).astype(f32)
                    q3 = last - q1 - q2
                    tail = jnp.where(
                        sub < 3,
                        q1,
                        jnp.where(sub < 5, q2, jnp.where(sub == 5, q3, 0.0)),
                    )
                    tops, lows = [], []
                    for c in range(3):
                        colour = jnp.where(
                            diagonal, jnp.broadcast_to(rest[1 + c : 2 + c], (8, 128)), 0.0
                        )
                        top = colour.astype(bf16).astype(f32)
                        tops.append(top)
                        lows.append(colour - top)
                    stack = jnp.concatenate(
                        [p1, p1, p1, p2, p2, p3, tail] + tops + tops + lows, axis=0
                    )
                    lhs[pl.ds(at, 128), :] = stack.T.astype(bf16)
                    colours[:, pl.ds(at, 128)] = jnp.concatenate(tops + lows, axis=0).astype(bf16)
                return carry

            lax.fori_loop(0, 2, gather_part, 0)

        def forward(chunk, carry):
            passing, picture = carry
            at = pl.multiple_of(chunk * CHUNK, CHUNK)
            power = jnp.dot(lhs[pl.ds(at, CHUNK), :], front[...], preferred_element_type=f32)
            alpha = jnp.exp2(power)
            alpha_ref[pl.ds(at, CHUNK), :] = alpha
            pieces = []
            for k in range(CHUNK_K):
                piece = alpha[8 * k : 8 * k + 8] * passing
                passing = passing - piece
                pieces.append(piece)
            weight = jnp.concatenate(pieces, axis=0)
            weight_ref[pl.ds(at, CHUNK), :] = weight
            high, low = halves(weight)
            high_ref[pl.ds(at, CHUNK), :] = high
            low_ref[pl.ds(at, CHUNK), :] = low
            own = colours[:, pl.ds(at, CHUNK)]
            picture = picture + jnp.dot(own, high, preferred_element_type=f32)
            picture = picture + jnp.dot(own, low, preferred_element_type=f32)
            return passing, picture

        _, picture = lax.fori_loop(
            0, CHUNKS, forward, (jnp.ones((8, PIX), f32), jnp.zeros((48, PIX), f32))
        )
        picture = picture[0:24] + picture[24:48]
        errors = []
        for c in range(3):
            image = picture[8 * c : 8 * c + 8]
            images[pl.ds(start, GROUP), c, :] = image
            errors.append(image - target[pl.ds(start, GROUP), c, :])
        for error in errors:
            square = error * error
            loss = loss + square[:, 0:128] + square[:, 128:256]
        error = jnp.concatenate(errors, axis=0)
        top = error.astype(bf16).astype(f32)
        bottom = error - top
        right = jnp.concatenate([jnp.zeros((56, PIX), f32), top, bottom, top], axis=0)
        right = right.astype(bf16)
        errs = jnp.concatenate([top, bottom], axis=0).astype(bf16)

        def backward(step, behind):
            at = pl.multiple_of((CHUNKS - 1 - step) * CHUNK, CHUNK)
            gain = jnp.dot(lhs[pl.ds(at, CHUNK), :], right, preferred_element_type=f32)
            alpha = alpha_ref[pl.ds(at, CHUNK), :]
            weight = weight_ref[pl.ds(at, CHUNK), :]
            pieces = [None] * CHUNK_K
            for k in reversed(range(CHUNK_K)):
                rows = slice(8 * k, 8 * k + 8)
                gap = gain[rows] - behind
                pieces[k] = weight[rows] * gap
                behind = behind + alpha[rows] * gap
            high, low = halves(jnp.concatenate(pieces, axis=0))
            contract = (((1,), (1,)), ((), ()))
            shape = lax.dot_general(back[...], high, contract, preferred_element_type=f32)
            shape = shape + lax.dot_general(back[...], low, contract, preferred_element_type=f32)
            shape = shape[0:16] + shape[16:32]
            paint = lax.dot_general(
                errs, high_ref[pl.ds(at, CHUNK), :], contract, preferred_element_type=f32
            )
            paint = paint + lax.dot_general(
                errs, low_ref[pl.ds(at, CHUNK), :], contract, preferred_element_type=f32
            )
            paint = paint[0:24] + paint[24:48]
            second = shape[8:16]
            row = iota((8, CHUNK), 0)
            for c in range(3):
                own = jnp.where(diag_wide, paint[8 * c : 8 * c + 8], 0.0)
                own = jnp.sum(own, axis=0, keepdims=True)
                second = jnp.where(row == 1 + c, jnp.broadcast_to(own, (8, CHUNK)), second)
            found = jnp.concatenate([shape[0:8], second], axis=0)
            high, low = halves(found)
            grads[0, :, pl.ds(at, CHUNK)] = high
            grads[1, :, pl.ds(at, CHUNK)] = low
            return behind

        lax.fori_loop(0, CHUNKS, backward, jnp.zeros((8, PIX), f32))

        def scatter(step, carry):
            at = pl.multiple_of(step * SCAT, SCAT)
            ids = ids_ref[:, pl.ds(at, SCAT)]
            block = lax.shift_right_logical(ids, 8)
            spot = ids & 255
            high = grads[0, :, pl.ds(at, SCAT)]
            low = grads[1, :, pl.ds(at, SCAT)]
            tops, lows = [], []
            for h in range(32):
                mask = jnp.where(block == h, 1.0, 0.0)
                mask = jnp.concatenate([mask, mask], axis=0).astype(bf16)
                tops.append(mask * high)
                lows.append(mask * low)
            left = jnp.concatenate(
                [jnp.concatenate(tops, axis=0), jnp.concatenate(lows, axis=0)], axis=1
            )
            row = iota((8, SCAT), 0)
            hot = jnp.concatenate(
                [jnp.where(spot == row + 8 * s, 1.0, 0.0) for s in range(32)], axis=0
            ).astype(bf16)
            hot = jnp.concatenate([hot, hot], axis=1)
            total[...] += lax.dot_general(
                left, hot, (((1,), (1,)), ((), ())), preferred_element_type=f32
            )
            return carry

        lax.fori_loop(0, ROWS // SCAT, scatter, 0)
        return loss

    loss = lax.fori_loop(0, GROUPS, one_group, jnp.zeros((8, 128), f32))
    for owner in range(OWNERS):
        for j in range(4):
            base = 16 * (2 * owner + j // 2)
            lanes = slice(128 * (j % 2), 128 * (j % 2) + 128)
            answer[owner, 8 * j : 8 * j + 8, :] = total[base : base + 8, lanes]
            answer[owner, 32 + 4 * j : 36 + 4 * j, :] = total[base + 8 : base + 12, lanes]
        answer[owner, 48:56, :] = loss


def collect_kernel(back, wanted, aux, out, loss, total):
    total[...] = jnp.zeros_like(total)

    def one_band(band, squares):
        tops, lows, blocks, spots = [], [], [], []
        for j in range(4):
            value = jnp.concatenate(
                [
                    back[band, 8 * j : 8 * j + 8, :],
                    back[band, 32 + 4 * j : 36 + 4 * j, :],
                    jnp.zeros((4, 128), f32),
                ],
                axis=0,
            )
            high, low = halves(value)
            tops.append(high)
            lows.append(low)
            ids = jnp.broadcast_to(wanted[band, j : j + 1, :], (8, 128))
            blocks.append(lax.shift_right_logical(ids, 8))
            spots.append(ids & 255)
        high = jnp.concatenate(tops, axis=1)
        low = jnp.concatenate(lows, axis=1)
        block = jnp.concatenate(blocks, axis=1)
        spot = jnp.concatenate(spots, axis=1)
        left_top, left_low = [], []
        for h in range(16):
            mask = jnp.where(block == h, 1.0, 0.0)
            mask = jnp.concatenate([mask, mask], axis=0).astype(bf16)
            left_top.append(mask * high)
            left_low.append(mask * low)
        left = jnp.concatenate(
            [jnp.concatenate(left_top, axis=0), jnp.concatenate(left_low, axis=0)], axis=1
        )
        row = iota((8, CAP), 0)
        hot = jnp.concatenate(
            [jnp.where(spot == row + 8 * s, 1.0, 0.0) for s in range(32)], axis=0
        ).astype(bf16)
        hot = jnp.concatenate([hot, hot], axis=1)
        total[...] += lax.dot_general(
            left, hot, (((1,), (1,)), ((), ())), preferred_element_type=f32
        )
        return squares + back[band, 48:56, :]

    squares = lax.fori_loop(0, OWNERS, one_band, jnp.zeros((8, 128), f32))
    whole = jnp.sum(jnp.sum(squares, axis=1, keepdims=True), axis=0, keepdims=True)
    loss[...] = whole * (1.0 / (TILES * OWNERS * PIX * 3))
    for h in range(16):
        lanes = slice(256 * h, 256 * h + 256)
        gain = [total[16 * h + c : 16 * h + c + 1, :] for c in range(12)]
        ca, sa, cb, sb, c0, c1, c2 = [aux[c : c + 1, lanes] for c in range(7)]
        cos_x, sin_x = 1.0 - 2.0 * sa * sa, 2.0 * sa * ca
        cos_y, sin_y = 1.0 - 2.0 * sb * sb, 2.0 * sb * cb
        d0 = (0.5 * KAPPA) * (cos_x * gain[1] + sin_x * gain[2] - gain[0])
        d2 = (0.5 * KAPPA) * (cos_y * gain[3] + sin_y * gain[4] - gain[0])
        cacb, casb, sacb, sasb = ca * cb, ca * sb, sa * cb, sa * sb
        d1 = (2.0 * KAPPA) * (casb * gain[6] - cacb * gain[5] + sacb * gain[7] - sasb * gain[8])
        twist = (2.0 * KAPPA) * c1
        da = KAPPA * c0 * (cos_x * gain[2] - sin_x * gain[1]) + twist * (
            sacb * gain[5] - sasb * gain[6] + cacb * gain[7] - casb * gain[8]
        )
        db = KAPPA * c2 * (cos_y * gain[4] - sin_y * gain[3]) + twist * (
            casb * gain[5] + cacb * gain[6] - sasb * gain[7] - sacb * gain[8]
        )
        out[0:1, lanes] = TURN * da
        out[1:2, lanes] = TURN * db
        out[2:3, lanes] = -(c0 * c0 * d0 + c0 * c1 * d1 + c1 * c1 * d2)
        out[3:4, lanes] = -(c0 * c1 * d0 + 0.5 * (c0 * c2 + c1 * c1) * d1 + c1 * c2 * d2)
        out[4:5, lanes] = -(c1 * c1 * d0 + c1 * c2 * d1 + c2 * c2 * d2)
        for c in range(3):
            raw = aux[7 + c : 8 + c, lanes]
            share = jnp.where(raw > 0.0, 1.0, jnp.where(raw == 0.0, 0.5, 0.0))
            out[5 + c : 6 + c, lanes] = share * gain[9 + c]
        spot = LOCAL + 256 * (h % 2)
        out[h // 2 : h // 2 + 1, spot : spot + 256] = gain[0]
    out[:, LOCAL + 512 :] = aux[0:8, LOCAL : LOCAL + 128]


def finish_kernel(
    gathered, log_scales, rotations, logit, grad_pos, grad_log, grad_rot, grad_op, grad_sh, work
):
    coef = jnp.concatenate([gathered[view, :, LOCAL + 512 :] for view in range(VIEWS)], axis=0)
    high, low = halves(coef.T)
    left = jnp.concatenate([high, low, high], axis=1)[0:64]
    for block in range(LOCAL // 512):
        lanes = slice(512 * block, 512 * block + 512)
        value = jnp.concatenate([gathered[view, :, lanes] for view in range(VIEWS)], axis=0)
        top, bottom = halves(value)
        right = jnp.concatenate([top, top, bottom], axis=0)
        work[:, lanes] = jnp.dot(left, right, preferred_element_type=f32)
    grad_sh[...] = work[0:48, :]
    grad_pos[...] = work[48:51, :]
    shade = gathered[0, :, LOCAL : LOCAL + 512]
    for view in range(1, VIEWS):
        shade = shade + gathered[view, :, LOCAL : LOCAL + 512]
    shade = jnp.concatenate([shade[s : s + 1, :] for s in range(8)], axis=1)
    grad_op[...] = shade / (1.0 + jnp.exp(logit[...]))
    k00, k01, k02, k11, k12, k22 = [work[51 + i : 52 + i, :] for i in range(6)]
    spread = [[k00, k01, k02], [k01, k11, k12], [k02, k12, k22]]
    inverse, (w, x, y, z), matrix = rotation([rotations[i : i + 1, :] for i in range(4)])
    d = [[None] * 3 for _ in range(3)]
    for j in range(3):
        scale = jnp.exp(log_scales[j : j + 1, :])
        square = scale * scale
        grad = None
        for i in range(3):
            value = (
                spread[i][0] * matrix[0][j]
                + spread[i][1] * matrix[1][j]
                + spread[i][2] * matrix[2][j]
            ) * square
            d[i][j] = value
            term = value * matrix[i][j]
            grad = term if grad is None else grad + term
        grad_log[j : j + 1, :] = grad
    dw = 2.0 * (x * (d[2][1] - d[1][2]) + y * (d[0][2] - d[2][0]) + z * (d[1][0] - d[0][1]))
    dx = 2.0 * (
        y * (d[0][1] + d[1][0])
        + z * (d[0][2] + d[2][0])
        + w * (d[2][1] - d[1][2])
        - 2.0 * x * (d[1][1] + d[2][2])
    )
    dy = 2.0 * (
        x * (d[0][1] + d[1][0])
        + z * (d[1][2] + d[2][1])
        + w * (d[0][2] - d[2][0])
        - 2.0 * y * (d[0][0] + d[2][2])
    )
    dz = 2.0 * (
        x * (d[0][2] + d[2][0])
        + y * (d[1][2] + d[2][1])
        + w * (d[1][0] - d[0][1])
        - 2.0 * z * (d[0][0] + d[1][1])
    )
    along = w * dw + x * dx + y * dy + z * dz
    for at, (part, unit) in enumerate(((dw, w), (dx, x), (dy, y), (dz, z))):
        grad_rot[at : at + 1, :] = (part - unit * along) * inverse


def whole():
    return pl.BlockSpec(memory_space=pltpu.VMEM)


def params(mega):
    return pltpu.CompilerParams(vmem_limit_bytes=mega << 20)


def shape(*dims):
    return jax.ShapeDtypeStruct(dims, f32)


def local(
    positions,
    log_scales,
    rotations,
    opacity_logit,
    sh_coeffs,
    view_angles,
    target,
    fetch_index,
    tile_slots,
    depth_order,
    block_count,
):
    wanted = lax.all_to_all(
        fetch_index.reshape(OWNERS, 4, 128), "band", split_axis=0, concat_axis=0, tiled=True
    )
    azimuth, elevation = view_angles[0, 0], view_angles[0, 1]
    cam = jnp.stack(
        [jnp.cos(azimuth), jnp.sin(azimuth), jnp.cos(elevation), jnp.sin(elevation)]
    ).reshape(1, 4)
    counts = jnp.tile(block_count.reshape(GROUPS, GROUP), (1, 16))
    front, back = pixel_tables()
    send, aux = pl.pallas_call(
        project_kernel,
        out_shape=(shape(OWNERS, SEND_ROWS, 128), shape(16, LOCAL + 128)),
        in_specs=[pl.BlockSpec(memory_space=pltpu.SMEM)] + [whole()] * 6,
        out_specs=(whole(), whole()),
        scratch_shapes=[pltpu.VMEM((16, LOCAL), f32)],
        compiler_params=params(32),
        name="project",
    )(cam, wanted, positions, log_scales, rotations, opacity_logit, sh_coeffs)
    table = lax.all_to_all(send, "band", split_axis=0, concat_axis=0, tiled=True)
    images, answer = pl.pallas_call(
        blend_kernel,
        out_shape=(shape(TILES, 3, PIX), shape(OWNERS, BACK_ROWS, 128)),
        in_specs=[whole()] * 7,
        out_specs=(whole(), whole()),
        scratch_shapes=[
            pltpu.VMEM((ROWS, 128), bf16),
            pltpu.VMEM((48, ROWS), bf16),
            pltpu.VMEM((ROWS, PIX), f32),
            pltpu.VMEM((ROWS, PIX), f32),
            pltpu.VMEM((ROWS, PIX), bf16),
            pltpu.VMEM((ROWS, PIX), bf16),
            pltpu.VMEM((8, ROWS), jnp.int32),
            pltpu.VMEM((2, 16, ROWS), bf16),
            pltpu.VMEM((512, 256), f32),
        ],
        compiler_params=params(48),
        name="blend",
    )(
        table,
        tile_slots[0],
        depth_order[0],
        counts,
        target[0],
        jnp.asarray(front),
        jnp.asarray(back),
    )
    returned = lax.all_to_all(answer, "band", split_axis=0, concat_axis=0, tiled=True)
    share, loss = pl.pallas_call(
        collect_kernel,
        out_shape=(shape(8, WIDE), shape(1, 1)),
        in_specs=[whole()] * 3,
        out_specs=(whole(), whole()),
        scratch_shapes=[pltpu.VMEM((256, 256), f32)],
        compiler_params=params(32),
        name="collect",
    )(returned, wanted, aux)
    gathered = lax.all_gather(share, "view", axis=0, tiled=False)
    grads = pl.pallas_call(
        finish_kernel,
        out_shape=(
            shape(3, LOCAL),
            shape(3, LOCAL),
            shape(4, LOCAL),
            shape(1, LOCAL),
            shape(48, LOCAL),
        ),
        in_specs=[whole()] * 4,
        out_specs=(whole(),) * 5,
        scratch_shapes=[pltpu.VMEM((64, LOCAL), f32)],
        compiler_params=params(32),
        name="finish",
    )(gathered, log_scales, rotations, opacity_logit)
    return (images[None], loss.reshape(1)) + tuple(grads)


def solution(mesh):
    in_specs = (
        P(None, "band"),
        P(None, "band"),
        P(None, "band"),
        P(None, "band"),
        P(None, "band"),
        P("view", None),
        P("view", "band", None, None),
        P("view", "band", None, None),
        P("view", "band", None),
        P("view", "band", None),
        P("view", "band"),
    )
    out_specs = (
        P("view", "band", None, None),
        P("view"),
        P(None, "band"),
        P(None, "band"),
        P(None, "band"),
        P(None, "band"),
        P(None, "band"),
    )
    return jax.shard_map(local, mesh=mesh, in_specs=in_specs, out_specs=out_specs, check_vma=False)
```

```python
import math

import jax
import jax.numpy as jnp
import ml_dtypes
import numpy as np
from jax import lax
from jax.experimental import pallas as pl
from jax.experimental.pallas import tpu as pltpu
from jax.sharding import PartitionSpec as P

SIDE = 16
PIX = SIDE * SIDE
SLOTS = 256
TILES = 48
CAP = 512
OWNERS = 16
LOCAL = 4096
VIEWS = 8
GROUP = 8
GROUPS = TILES // GROUP
ROWS = GROUP * SLOTS
CHUNK = 256
CHUNK_K = CHUNK // GROUP
CHUNKS = ROWS // CHUNK
SCAT = 512
TOGETHER = 3
UNROLL_GATHER = 4
UNROLL_FORWARD = 4
UNROLL_BACKWARD = 8
UNROLL_SCATTER = 4
UNROLL_SELECT = 4
UNROLL_COLLECT = 4
TURN = 2.0 * math.pi / SIDE
KAPPA = 0.5 / (TURN * TURN)
LOG2E = 1.4426950408889634
DEAD = -1024.0
SEND_ROWS = 48
BACK_ROWS = 56
WIDE = LOCAL + 512 + 128

f32 = jnp.float32
bf16 = jnp.bfloat16

zero_term = 0.28209479177387814
first_term = 0.4886025119029199
second_terms = (
    1.0925484305920792,
    -1.0925484305920792,
    0.31539156525252005,
    -1.0925484305920792,
    0.5462742152960396,
)
third_terms = (
    -0.5900435899266435,
    2.890611442640554,
    -0.4570457994644658,
    0.3731763325901154,
    -0.4570457994644658,
    1.445305721320277,
    -0.5900435899266435,
)
dilation = 0.3


def pixel_tables():
    pixel = np.arange(PIX)
    ang_x = TURN * (pixel % SIDE + 0.5)
    ang_y = TURN * (pixel // SIDE + 0.5)
    sx, cx, sy, cy = np.sin(ang_x), np.cos(ang_x), np.sin(ang_y), np.cos(ang_y)
    rows = np.stack(
        [
            np.ones(PIX),
            np.cos(2 * ang_x),
            np.sin(2 * ang_x),
            np.cos(2 * ang_y),
            np.sin(2 * ang_y),
            sx * sy,
            sx * cy,
            cx * sy,
            cx * cy,
        ]
    )
    kind = ml_dtypes.bfloat16
    parts = []
    rest = rows
    for _ in range(3):
        part = rest.astype(kind)
        parts.append(part)
        rest = rest - part.astype(np.float64)
    order = (0, 1, 2, 0, 1)
    front = np.zeros((128, PIX), kind)
    for at, which in enumerate(order):
        front[8 * at : 8 * at + 8] = parts[which][:8]
        front[40 + at] = parts[which][8]
    back = np.zeros((32, PIX), kind)
    back[0:9] = parts[0]
    back[16:25] = parts[1]
    return front, back


def harmonic_basis(dir_x, dir_y, dir_z):
    square_x = dir_x * dir_x
    square_y = dir_y * dir_y
    square_z = dir_z * dir_z
    return [
        zero_term + 0.0 * dir_x,
        -first_term * dir_y,
        first_term * dir_z,
        -first_term * dir_x,
        second_terms[0] * dir_x * dir_y,
        second_terms[1] * dir_y * dir_z,
        second_terms[2] * (2.0 * square_z - square_x - square_y),
        second_terms[3] * dir_x * dir_z,
        second_terms[4] * (square_x - square_y),
        third_terms[0] * dir_y * (3.0 * square_x - square_y),
        third_terms[1] * dir_x * dir_y * dir_z,
        third_terms[2] * dir_y * (4.0 * square_z - square_x - square_y),
        third_terms[3] * dir_z * (2.0 * square_z - 3.0 * square_x - 3.0 * square_y),
        third_terms[4] * dir_x * (4.0 * square_z - square_x - square_y),
        third_terms[5] * dir_z * (square_x - square_y),
        third_terms[6] * dir_x * (square_x - 3.0 * square_y),
    ]


def iota(shape, axis):
    return lax.broadcasted_iota(jnp.int32, shape, axis)


def wave(mean):
    cycles = mean * (1.0 / SIDE)
    part = cycles - jnp.floor(cycles + 0.5)
    x = part * math.pi
    x2 = x * x
    sine = 1.0 / 6227020800.0
    for scale in (-1.0 / 39916800.0, 1.0 / 362880.0, -1.0 / 5040.0, 1.0 / 120.0, -1.0 / 6.0, 1.0):
        sine = sine * x2 + scale
    sine = sine * x
    cosine = -1.0 / 87178291200.0
    for scale in (
        1.0 / 479001600.0,
        -1.0 / 3628800.0,
        1.0 / 40320.0,
        -1.0 / 720.0,
        1.0 / 24.0,
        -0.5,
        1.0,
    ):
        cosine = cosine * x2 + scale
    return 2.0 * sine * cosine, 1.0 - 2.0 * sine * sine


def rotation(rows):
    length = jnp.sqrt(
        rows[0] * rows[0] + rows[1] * rows[1] + rows[2] * rows[2] + rows[3] * rows[3]
    )
    inverse = 1.0 / length
    w, x, y, z = [row * inverse for row in rows]
    matrix = [
        [1.0 - 2.0 * (y * y + z * z), 2.0 * (x * y - w * z), 2.0 * (x * z + w * y)],
        [2.0 * (x * y + w * z), 1.0 - 2.0 * (x * x + z * z), 2.0 * (y * z - w * x)],
        [2.0 * (x * z - w * y), 2.0 * (y * z + w * x), 1.0 - 2.0 * (x * x + y * y)],
    ]
    return inverse, (w, x, y, z), matrix


def halves(value):
    high = value.astype(bf16)
    low = (value - high.astype(f32)).astype(bf16)
    return high, low


def pick(table, lanes):
    return jnp.take_along_axis(table, lanes, axis=1)


def project_kernel(cam, positions, log_scales, rotations, logit, sh, parts, aux, tab):
    cos_a, sin_a, cos_e, sin_e = cam[0, 0], cam[0, 1], cam[0, 2], cam[0, 3]
    right = (-sin_a, cos_a)
    upward = (-sin_e * cos_a, -sin_e * sin_a, cos_e)
    basis = harmonic_basis(cos_e * cos_a, cos_e * sin_a, sin_e)
    pos = [positions[i : i + 1, :] for i in range(3)]
    mean_x = right[0] * pos[0] + right[1] * pos[1]
    mean_y = upward[0] * pos[0] + upward[1] * pos[1] + upward[2] * pos[2]
    _, _, matrix = rotation([rotations[i : i + 1, :] for i in range(4)])
    scales = [jnp.exp(log_scales[i : i + 1, :]) for i in range(3)]
    first = [(right[0] * matrix[0][j] + right[1] * matrix[1][j]) * scales[j] for j in range(3)]
    second = [
        (upward[0] * matrix[0][j] + upward[1] * matrix[1][j] + upward[2] * matrix[2][j])
        * scales[j]
        for j in range(3)
    ]
    cov_a = first[0] * first[0] + first[1] * first[1] + first[2] * first[2] + dilation
    cov_b = first[0] * second[0] + first[1] * second[1] + first[2] * second[2]
    cov_c = second[0] * second[0] + second[1] * second[1] + second[2] * second[2] + dilation
    inverse = 1.0 / (cov_a * cov_c - cov_b * cov_b)
    c0, c1, c2 = cov_c * inverse, -cov_b * inverse, cov_a * inverse
    sa, ca = wave(mean_x)
    sb, cb = wave(mean_y)
    unit = KAPPA * LOG2E
    g0 = -LOG2E * jnp.log(1.0 + jnp.exp(-logit[...])) - (0.5 * unit) * (c0 + c2)
    cross = (-2.0 * unit) * c1
    half_x, half_y = (0.5 * unit) * c0, (0.5 * unit) * c2
    features = [
        g0,
        half_x * (1.0 - 2.0 * sa * sa),
        half_x * (2.0 * sa * ca),
        half_y * (1.0 - 2.0 * sb * sb),
        half_y * (2.0 * sb * cb),
        cross * ca * cb,
        -cross * ca * sb,
        -cross * sa * cb,
        cross * sa * sb,
    ]
    row48 = iota((48, 128), 0)
    weight = jnp.zeros((48, 128), f32)
    for k in range(16):
        weight = jnp.where(row48 // 3 == k, basis[k], weight)
    residue = row48 % 3
    masks = [jnp.where(residue == c, weight, 0.0) for c in range(3)]
    for block in range(LOCAL // 128):
        lanes = slice(128 * block, 128 * block + 128)
        piece = sh[:, lanes]
        for c in range(3):
            raw = 0.5 + jnp.sum(masks[c] * piece, axis=0, keepdims=True)
            aux[7 + c : 8 + c, lanes] = raw
            tab[9 + c : 10 + c, lanes] = jnp.maximum(raw, 0.0)
    for at, row in enumerate(features):
        tab[at : at + 1, :] = row
    for at, row in enumerate((ca, sa, cb, sb, c0, c1, c2)):
        aux[at : at + 1, 0:LOCAL] = row
    aux[10:16, 0:LOCAL] = jnp.zeros((6, LOCAL), f32)
    lane = iota((8, 128), 1)
    sub = iota((8, 128), 0)
    coef = jnp.zeros((8, 128), f32)
    for k in range(16):
        coef = jnp.where((lane // 3 == k) & (sub == 5 + lane % 3), basis[k], coef)

    def put(base, row, at, value):
        return jnp.where((sub == row) & (lane == at), value, base)

    for i in range(3):
        if i < 2:
            coef = put(coef, 0, 48 + i, right[i])
        coef = put(coef, 1, 48 + i, upward[i])
    at = 51
    for i in range(3):
        for j in range(i, 3):
            if j < 2:
                coef = put(coef, 2, at, 2.0 * right[i] * right[j])
            mixed = 0.0
            if i < 2:
                mixed = mixed + right[i] * upward[j]
            if j < 2:
                mixed = mixed + right[j] * upward[i]
            if i < 2 or j < 2:
                coef = put(coef, 3, at, 2.0 * mixed)
            coef = put(coef, 4, at, 2.0 * upward[i] * upward[j])
            at += 1
    aux[0:8, LOCAL : LOCAL + 128] = coef
    aux[8:16, LOCAL : LOCAL + 128] = jnp.zeros((8, 128), f32)

    for h in range(16):
        lanes = slice(256 * h, 256 * h + 256)
        value = tab[0:8, lanes]
        rest = tab[8:12, lanes]
        top = value.astype(bf16).astype(f32)
        peak = rest.astype(bf16).astype(f32)
        stack = jnp.concatenate([top, value - top, peak, rest - peak], axis=0)
        if h % 2 == 0:
            before = stack
        else:
            both = jnp.concatenate([before, stack], axis=0)
            parts[24 * h - 24 : 24 * h + 24, :] = both.astype(bf16)


def unit_rows(spot, width):
    row = iota((16, width), 0).astype(f32)
    one, zero = jnp.ones((16, width), bf16), jnp.zeros((16, width), bf16)
    return jnp.concatenate(
        [jnp.where(spot == (row + 16.0 * s).astype(bf16), one, zero) for s in range(16)], axis=0
    )


def small(ids):
    wide = ids.astype(f32)
    return jnp.concatenate([wide, wide], axis=0).astype(bf16)


def masked_rows(block, count, high, low):
    none = jnp.zeros_like(high)
    tops, lows = [], []
    for h in range(count):
        mask = block == jnp.full(block.shape, h, bf16)
        tops.append(jnp.where(mask, high, none))
        lows.append(jnp.where(mask, low, none))
    return jnp.concatenate(
        [jnp.concatenate(tops, axis=0), jnp.concatenate(lows, axis=0)], axis=1
    )


def select_kernel(wanted, parts, send):
    def one_band(band, carry):
        ids = jnp.concatenate(
            [jnp.broadcast_to(wanted[band, j : j + 1, :], (8, 128)) for j in range(4)], axis=1
        )
        block = lax.shift_right_logical(ids, 8)
        hot = unit_rows(small(ids & 255), CAP)
        found = jnp.dot(parts[...], hot, preferred_element_type=f32)
        acc = [jnp.zeros((8, CAP), f32)] * 3
        for h in range(16):
            mask = block == h
            for part in range(3):
                start = 24 * h + 8 * part
                acc[part] = jnp.where(mask, found[start : start + 8], acc[part])
        value = acc[0] + acc[1]
        rest = acc[2] + pltpu.roll(acc[2], 4, 0)
        for j in range(4):
            lanes = slice(128 * j, 128 * j + 128)
            send[band, 8 * j : 8 * j + 8, :] = value[:, lanes]
            send[band, 32 + 4 * j : 36 + 4 * j, :] = rest[0:4, lanes]
        return carry

    lax.fori_loop(0, OWNERS, one_band, 0, unroll=UNROLL_SELECT)


def blend_kernel(
    table,
    slots,
    order,
    counts,
    target,
    front,
    back,
    images,
    answer,
    tab,
    lhs,
    colours,
    alpha_ref,
    weight_ref,
    high_ref,
    low_ref,
    hot_ref,
    block_ref,
    grads,
    total,
):
    lane = iota((8, 128), 1)
    sub = iota((8, 128), 0)
    diagonal = sub == (lane & 7)
    diag_wide = iota((8, CHUNK), 0) == (iota((8, CHUNK), 1) & 7)
    depth = lax.shift_right_logical(lane, 3)
    total[...] = jnp.zeros_like(total)
    for owner in range(OWNERS):
        pieces = []
        for part in range(2):
            tops, lows = [], []
            for j in (2 * part, 2 * part + 1):
                value = table[owner, 8 * j : 8 * j + 8, :]
                rest = table[owner, 32 + 4 * j : 36 + 4 * j, :]
                top = value.astype(bf16).astype(f32)
                peak = rest.astype(bf16).astype(f32)
                tops.append(jnp.concatenate([top, value - top, peak, rest - peak], axis=0))
            pieces.append(jnp.concatenate(tops, axis=1))
        tab[48 * owner : 48 * owner + 48, :] = jnp.concatenate(pieces, axis=0).astype(bf16)

    def one_set(index, loss):
        groups = [index * TOGETHER + g for g in range(TOGETHER)]
        starts = [pl.multiple_of(group * GROUP, GROUP) for group in groups]
        limits, ordered = [], []
        for g in range(TOGETHER):
            limits.append(jnp.broadcast_to(counts[pl.ds(groups[g], 1), :], (8, 128)))
            own = slots[pl.ds(starts[g], GROUP), :]
            sequence = order[pl.ds(starts[g], GROUP), :]
            for half in range(2):
                seq = sequence[:, 128 * half : 128 * half + 128]
                spot = seq & 127
                ordered.append(
                    jnp.where(seq < 128, pick(own[:, 0:128], spot), pick(own[:, 128:256], spot))
                )

        def gather(chunk, carry):
            at = pl.multiple_of(chunk * CHUNK, CHUNK)
            for g in range(TOGETHER):
                values = []
                for j in range(2):
                    base = (2 * chunk + j) * 16 + depth
                    value = jnp.where(
                        base < 128,
                        pick(ordered[2 * g], base & 127),
                        pick(ordered[2 * g + 1], base & 127),
                    )
                    value = jnp.sum(jnp.where(diagonal, value, 0), axis=0, keepdims=True)
                    values.append(jnp.broadcast_to(value, (8, 128)))
                ids = jnp.concatenate(values, axis=1)
                block = lax.shift_right_logical(ids, 8)
                hot = unit_rows(small(ids & 255), CHUNK)
                hot_ref[g, :, pl.ds(at, CHUNK)] = hot
                block_ref[g, :, pl.ds(at, CHUNK)] = small(block)
                found = jnp.dot(tab[...], hot, preferred_element_type=f32)
                acc = [jnp.zeros((8, CHUNK), f32)] * 3
                for h in range(32):
                    mask = block == h
                    for part in range(3):
                        start = 24 * h + 8 * part
                        acc[part] = jnp.where(mask, found[start : start + 8], acc[part])
                base = chunk * CHUNK_K + lax.shift_right_logical(iota((8, CHUNK), 1), 3)
                limit = jnp.concatenate([limits[g], limits[g]], axis=1)
                line = iota((8, CHUNK), 0)
                p1 = jnp.where((base >= limit) & (line == 0), DEAD, acc[0])
                p2 = acc[1]

                def spread(which):
                    return jnp.broadcast_to(acc[2][which : which + 1], (8, CHUNK))

                tail = jnp.where(line < 3, spread(0), jnp.where(line < 5, spread(4), 0.0))
                tops = [jnp.where(diag_wide, spread(1 + c), 0.0) for c in range(3)]
                lows = [jnp.where(diag_wide, spread(5 + c), 0.0) for c in range(3)]
                blank = jnp.zeros((8, CHUNK), f32)
                stack = jnp.concatenate(
                    [p1, p1, p1, p2, p2, tail, blank] + tops + tops + lows, axis=0
                )
                lhs[g, pl.ds(at, CHUNK), :] = stack.T.astype(bf16)
                colours[g, :, pl.ds(at, CHUNK)] = jnp.concatenate(tops + lows, axis=0).astype(bf16)
            return carry

        lax.fori_loop(0, CHUNKS, gather, 0, unroll=UNROLL_GATHER)

        def forward(chunk, carry):
            at = pl.multiple_of(chunk * CHUNK, CHUNK)
            result = []
            for g in range(TOGETHER):
                passing, picture = carry[2 * g], carry[2 * g + 1]
                power = jnp.dot(
                    lhs[g, pl.ds(at, CHUNK), :], front[...], preferred_element_type=f32
                )
                alpha = jnp.exp2(power)
                alpha_ref[g, pl.ds(at, CHUNK), :] = alpha
                pieces = []
                for k in range(CHUNK_K):
                    piece = alpha[8 * k : 8 * k + 8] * passing
                    passing = passing - piece
                    pieces.append(piece)
                weight = jnp.concatenate(pieces, axis=0)
                weight_ref[g, pl.ds(at, CHUNK), :] = weight
                high, low = halves(weight)
                high_ref[g, pl.ds(at, CHUNK), :] = high
                low_ref[g, pl.ds(at, CHUNK), :] = low
                own = colours[g, :, pl.ds(at, CHUNK)]
                picture = picture + jnp.dot(own, high, preferred_element_type=f32)
                picture = picture + jnp.dot(own, low, preferred_element_type=f32)
                result += [passing, picture]
            return tuple(result)

        begin = (jnp.ones((8, PIX), f32), jnp.zeros((48, PIX), f32)) * TOGETHER
        done = lax.fori_loop(0, CHUNKS, forward, begin, unroll=UNROLL_FORWARD)
        rights, errs = [], []
        for g in range(TOGETHER):
            picture = done[2 * g + 1]
            picture = picture[0:24] + picture[24:48]
            errors = []
            for c in range(3):
                image = picture[8 * c : 8 * c + 8]
                images[pl.ds(starts[g], GROUP), c, :] = image
                errors.append(image - target[pl.ds(starts[g], GROUP), c, :])
            for error in errors:
                square = error * error
                loss = loss + square[:, 0:128] + square[:, 128:256]
            error = jnp.concatenate(errors, axis=0)
            top = error.astype(bf16).astype(f32)
            bottom = error - top
            right = jnp.concatenate([jnp.zeros((56, PIX), f32), top, bottom, top], axis=0)
            rights.append(right.astype(bf16))
            errs.append(jnp.concatenate([top, bottom], axis=0).astype(bf16))

        def backward(step, carry):
            at = pl.multiple_of((CHUNKS - 1 - step) * CHUNK, CHUNK)
            result = []
            for g in range(TOGETHER):
                behind = carry[g]
                gain = jnp.dot(
                    lhs[g, pl.ds(at, CHUNK), :], rights[g], preferred_element_type=f32
                )
                alpha = alpha_ref[g, pl.ds(at, CHUNK), :]
                weight = weight_ref[g, pl.ds(at, CHUNK), :]
                pieces = [None] * CHUNK_K
                for k in reversed(range(CHUNK_K)):
                    rows = slice(8 * k, 8 * k + 8)
                    gap = gain[rows] - behind
                    pieces[k] = weight[rows] * gap
                    behind = behind + alpha[rows] * gap
                result.append(behind)
                high, low = halves(jnp.concatenate(pieces, axis=0))
                contract = (((1,), (1,)), ((), ()))
                shape = lax.dot_general(back[...], high, contract, preferred_element_type=f32)
                shape = shape + lax.dot_general(
                    back[...], low, contract, preferred_element_type=f32
                )
                shape = shape[0:16] + shape[16:32]
                paint = lax.dot_general(
                    errs[g], high_ref[g, pl.ds(at, CHUNK), :], contract, preferred_element_type=f32
                )
                paint = paint + lax.dot_general(
                    errs[g], low_ref[g, pl.ds(at, CHUNK), :], contract, preferred_element_type=f32
                )
                paint = paint[0:24] + paint[24:48]
                second = shape[8:16]
                row = iota((8, CHUNK), 0)
                for c in range(3):
                    own = jnp.where(diag_wide, paint[8 * c : 8 * c + 8], 0.0)
                    own = jnp.sum(own, axis=0, keepdims=True)
                    second = jnp.where(row == 1 + c, jnp.broadcast_to(own, (8, CHUNK)), second)
                found = jnp.concatenate([shape[0:8], second], axis=0)
                high, low = halves(found)
                grads[g, 0, :, pl.ds(at, CHUNK)] = high
                grads[g, 1, :, pl.ds(at, CHUNK)] = low
            return tuple(result)

        lax.fori_loop(
            0,
            CHUNKS,
            backward,
            (jnp.zeros((8, PIX), f32),) * TOGETHER,
            unroll=UNROLL_BACKWARD,
        )

        def scatter(step, carry):
            at = pl.multiple_of(step * SCAT, SCAT)
            for g in range(TOGETHER):
                block = block_ref[g, :, pl.ds(at, SCAT)]
                high = grads[g, 0, :, pl.ds(at, SCAT)]
                low = grads[g, 1, :, pl.ds(at, SCAT)]
                left = masked_rows(block, 32, high, low)
                hot = hot_ref[g, :, pl.ds(at, SCAT)]
                hot = jnp.concatenate([hot, hot], axis=1)
                total[...] += lax.dot_general(
                    left, hot, (((1,), (1,)), ((), ())), preferred_element_type=f32
                )
            return carry

        lax.fori_loop(0, ROWS // SCAT, scatter, 0, unroll=UNROLL_SCATTER)
        return loss

    loss = lax.fori_loop(0, GROUPS // TOGETHER, one_set, jnp.zeros((8, 128), f32))
    for owner in range(OWNERS):
        for j in range(4):
            base = 16 * (2 * owner + j // 2)
            lanes = slice(128 * (j % 2), 128 * (j % 2) + 128)
            answer[owner, 8 * j : 8 * j + 8, :] = total[base : base + 8, lanes]
            answer[owner, 32 + 4 * j : 36 + 4 * j, :] = total[base + 8 : base + 12, lanes]
        answer[owner, 48:56, :] = loss


def blend_scratch():
    return [
        pltpu.VMEM((768, 256), bf16),
        pltpu.VMEM((TOGETHER, ROWS, 128), bf16),
        pltpu.VMEM((TOGETHER, 48, ROWS), bf16),
        pltpu.VMEM((TOGETHER, ROWS, PIX), f32),
        pltpu.VMEM((TOGETHER, ROWS, PIX), f32),
        pltpu.VMEM((TOGETHER, ROWS, PIX), bf16),
        pltpu.VMEM((TOGETHER, ROWS, PIX), bf16),
        pltpu.VMEM((TOGETHER, 256, ROWS), bf16),
        pltpu.VMEM((TOGETHER, 16, ROWS), bf16),
        pltpu.VMEM((TOGETHER, 2, 16, ROWS), bf16),
        pltpu.VMEM((512, 256), f32),
    ]


def collect_kernel(back, wanted, aux, out, loss, total):
    total[...] = jnp.zeros_like(total)

    def one_band(band, squares):
        tops, lows, blocks, spots = [], [], [], []
        for j in range(4):
            value = jnp.concatenate(
                [
                    back[band, 8 * j : 8 * j + 8, :],
                    back[band, 32 + 4 * j : 36 + 4 * j, :],
                    jnp.zeros((4, 128), f32),
                ],
                axis=0,
            )
            high, low = halves(value)
            tops.append(high)
            lows.append(low)
            ids = jnp.broadcast_to(wanted[band, j : j + 1, :], (8, 128))
            blocks.append(lax.shift_right_logical(ids, 8))
            spots.append(ids & 255)
        high = jnp.concatenate(tops, axis=1)
        low = jnp.concatenate(lows, axis=1)
        block = jnp.concatenate(blocks, axis=1)
        spot = jnp.concatenate(spots, axis=1)
        left = masked_rows(small(block), 16, high, low)
        hot = unit_rows(small(spot), CAP)
        hot = jnp.concatenate([hot, hot], axis=1)
        total[...] += lax.dot_general(
            left, hot, (((1,), (1,)), ((), ())), preferred_element_type=f32
        )
        return squares + back[band, 48:56, :]

    squares = lax.fori_loop(
        0, OWNERS, one_band, jnp.zeros((8, 128), f32), unroll=UNROLL_COLLECT
    )
    whole = jnp.sum(jnp.sum(squares, axis=1, keepdims=True), axis=0, keepdims=True)
    loss[...] = whole * (1.0 / (TILES * OWNERS * PIX * 3))
    for h in range(16):
        lanes = slice(256 * h, 256 * h + 256)
        gain = [total[16 * h + c : 16 * h + c + 1, :] for c in range(12)]
        ca, sa, cb, sb, c0, c1, c2 = [aux[c : c + 1, lanes] for c in range(7)]
        cos_x, sin_x = 1.0 - 2.0 * sa * sa, 2.0 * sa * ca
        cos_y, sin_y = 1.0 - 2.0 * sb * sb, 2.0 * sb * cb
        d0 = (0.5 * KAPPA) * (cos_x * gain[1] + sin_x * gain[2] - gain[0])
        d2 = (0.5 * KAPPA) * (cos_y * gain[3] + sin_y * gain[4] - gain[0])
        cacb, casb, sacb, sasb = ca * cb, ca * sb, sa * cb, sa * sb
        d1 = (2.0 * KAPPA) * (casb * gain[6] - cacb * gain[5] + sacb * gain[7] - sasb * gain[8])
        twist = (2.0 * KAPPA) * c1
        da = KAPPA * c0 * (cos_x * gain[2] - sin_x * gain[1]) + twist * (
            sacb * gain[5] - sasb * gain[6] + cacb * gain[7] - casb * gain[8]
        )
        db = KAPPA * c2 * (cos_y * gain[4] - sin_y * gain[3]) + twist * (
            casb * gain[5] + cacb * gain[6] - sasb * gain[7] - sacb * gain[8]
        )
        out[0:1, lanes] = TURN * da
        out[1:2, lanes] = TURN * db
        out[2:3, lanes] = -(c0 * c0 * d0 + c0 * c1 * d1 + c1 * c1 * d2)
        out[3:4, lanes] = -(c0 * c1 * d0 + 0.5 * (c0 * c2 + c1 * c1) * d1 + c1 * c2 * d2)
        out[4:5, lanes] = -(c1 * c1 * d0 + c1 * c2 * d1 + c2 * c2 * d2)
        for c in range(3):
            raw = aux[7 + c : 8 + c, lanes]
            share = jnp.where(raw > 0.0, 1.0, jnp.where(raw == 0.0, 0.5, 0.0))
            out[5 + c : 6 + c, lanes] = share * gain[9 + c]
        spot = LOCAL + 256 * (h % 2)
        out[h // 2 : h // 2 + 1, spot : spot + 256] = gain[0]
    out[:, LOCAL + 512 :] = aux[0:8, LOCAL : LOCAL + 128]


def finish_kernel(
    near, far, log_scales, rotations, logit, grad_pos, grad_log, grad_rot, grad_op, grad_sh, work
):
    gathered = [ref.at[i] for ref in (near, far) for i in range(VIEWS // 2)]
    coef = jnp.concatenate([gathered[view][:, LOCAL + 512 :] for view in range(VIEWS)], axis=0)
    high, low = halves(coef.T)
    left = jnp.concatenate([high, low, high], axis=1)[0:64]
    for block in range(LOCAL // 512):
        lanes = slice(512 * block, 512 * block + 512)
        value = jnp.concatenate([gathered[view][:, lanes] for view in range(VIEWS)], axis=0)
        top, bottom = halves(value)
        right = jnp.concatenate([top, top, bottom], axis=0)
        work[:, lanes] = jnp.dot(left, right, preferred_element_type=f32)
    grad_sh[...] = work[0:48, :]
    grad_pos[...] = work[48:51, :]
    shade = gathered[0][:, LOCAL : LOCAL + 512]
    for view in range(1, VIEWS):
        shade = shade + gathered[view][:, LOCAL : LOCAL + 512]
    shade = jnp.concatenate([shade[s : s + 1, :] for s in range(8)], axis=1)
    grad_op[...] = shade / (1.0 + jnp.exp(logit[...]))
    k00, k01, k02, k11, k12, k22 = [work[51 + i : 52 + i, :] for i in range(6)]
    spread = [[k00, k01, k02], [k01, k11, k12], [k02, k12, k22]]
    inverse, (w, x, y, z), matrix = rotation([rotations[i : i + 1, :] for i in range(4)])
    d = [[None] * 3 for _ in range(3)]
    for j in range(3):
        scale = jnp.exp(log_scales[j : j + 1, :])
        square = scale * scale
        grad = None
        for i in range(3):
            value = (
                spread[i][0] * matrix[0][j]
                + spread[i][1] * matrix[1][j]
                + spread[i][2] * matrix[2][j]
            ) * square
            d[i][j] = value
            term = value * matrix[i][j]
            grad = term if grad is None else grad + term
        grad_log[j : j + 1, :] = grad
    dw = 2.0 * (x * (d[2][1] - d[1][2]) + y * (d[0][2] - d[2][0]) + z * (d[1][0] - d[0][1]))
    dx = 2.0 * (
        y * (d[0][1] + d[1][0])
        + z * (d[0][2] + d[2][0])
        + w * (d[2][1] - d[1][2])
        - 2.0 * x * (d[1][1] + d[2][2])
    )
    dy = 2.0 * (
        x * (d[0][1] + d[1][0])
        + z * (d[1][2] + d[2][1])
        + w * (d[0][2] - d[2][0])
        - 2.0 * y * (d[0][0] + d[2][2])
    )
    dz = 2.0 * (
        x * (d[0][2] + d[2][0])
        + y * (d[1][2] + d[2][1])
        + w * (d[1][0] - d[0][1])
        - 2.0 * z * (d[0][0] + d[1][1])
    )
    along = w * dw + x * dx + y * dy + z * dz
    for at, (part, unit) in enumerate(((dw, w), (dx, x), (dy, y), (dz, z))):
        grad_rot[at : at + 1, :] = (part - unit * along) * inverse


def whole():
    return pl.BlockSpec(memory_space=pltpu.VMEM)


def params(mega):
    return pltpu.CompilerParams(vmem_limit_bytes=mega << 20)


def shape(*dims):
    return jax.ShapeDtypeStruct(dims, f32)


def local(
    positions,
    log_scales,
    rotations,
    opacity_logit,
    sh_coeffs,
    view_angles,
    target,
    fetch_index,
    tile_slots,
    depth_order,
    block_count,
):
    wanted = lax.all_to_all(
        fetch_index.reshape(OWNERS, 4, 128), "band", split_axis=0, concat_axis=0, tiled=True
    )
    azimuth, elevation = view_angles[0, 0], view_angles[0, 1]
    cam = jnp.stack(
        [jnp.cos(azimuth), jnp.sin(azimuth), jnp.cos(elevation), jnp.sin(elevation)]
    ).reshape(1, 4)
    counts = jnp.tile(block_count.reshape(GROUPS, GROUP), (1, 16))
    front, back = pixel_tables()
    parts, aux = pl.pallas_call(
        project_kernel,
        out_shape=(jax.ShapeDtypeStruct((384, 256), bf16), shape(16, LOCAL + 128)),
        in_specs=[pl.BlockSpec(memory_space=pltpu.SMEM)] + [whole()] * 5,
        out_specs=(whole(), whole()),
        scratch_shapes=[pltpu.VMEM((16, LOCAL), f32)],
        compiler_params=params(32),
        name="project",
    )(cam, positions, log_scales, rotations, opacity_logit, sh_coeffs)
    send = pl.pallas_call(
        select_kernel,
        out_shape=shape(OWNERS, SEND_ROWS, 128),
        in_specs=[whole()] * 2,
        out_specs=whole(),
        compiler_params=params(32),
        name="select",
    )(wanted, parts)
    table = lax.all_to_all(send, "band", split_axis=0, concat_axis=0, tiled=True)
    images, answer = pl.pallas_call(
        blend_kernel,
        out_shape=(shape(TILES, 3, PIX), shape(OWNERS, BACK_ROWS, 128)),
        in_specs=[whole()] * 7,
        out_specs=(whole(), whole()),
        scratch_shapes=blend_scratch(),
        compiler_params=params(48),
        name="blend",
    )(
        table,
        tile_slots[0],
        depth_order[0],
        counts,
        target[0],
        jnp.asarray(front),
        jnp.asarray(back),
    )
    returned = lax.all_to_all(answer, "band", split_axis=0, concat_axis=0, tiled=True)
    share, loss = pl.pallas_call(
        collect_kernel,
        out_shape=(shape(8, WIDE), shape(1, 1)),
        in_specs=[whole()] * 3,
        out_specs=(whole(), whole()),
        scratch_shapes=[pltpu.VMEM((256, 256), f32)],
        compiler_params=params(32),
        name="collect",
    )(returned, wanted, aux)
    around = [share]
    for step in (4, 2, 6):
        ring = [(v, (v + step) % VIEWS) for v in range(VIEWS)]
        around.append(lax.ppermute(share, "view", ring))
    near = jnp.stack(around)
    far = lax.ppermute(near, "view", [(v, v ^ 1) for v in range(VIEWS)])
    grads = pl.pallas_call(
        finish_kernel,
        out_shape=(
            shape(3, LOCAL),
            shape(3, LOCAL),
            shape(4, LOCAL),
            shape(1, LOCAL),
            shape(48, LOCAL),
        ),
        in_specs=[whole()] * 5,
        out_specs=(whole(),) * 5,
        scratch_shapes=[pltpu.VMEM((64, LOCAL), f32)],
        compiler_params=params(32),
        name="finish",
    )(near, far, log_scales, rotations, opacity_logit)
    return (images[None], loss.reshape(1)) + tuple(grads)


def solution(mesh):
    in_specs = (
        P(None, "band"),
        P(None, "band"),
        P(None, "band"),
        P(None, "band"),
        P(None, "band"),
        P("view", None),
        P("view", "band", None, None),
        P("view", "band", None, None),
        P("view", "band", None),
        P("view", "band", None),
        P("view", "band"),
    )
    out_specs = (
        P("view", "band", None, None),
        P("view"),
        P(None, "band"),
        P(None, "band"),
        P(None, "band"),
        P(None, "band"),
        P(None, "band"),
    )
    return jax.shard_map(local, mesh=mesh, in_specs=in_specs, out_specs=out_specs, check_vma=False)
```

```python
import math

import jax
import jax.numpy as jnp
import ml_dtypes
import numpy as np
from jax import lax
from jax.experimental import pallas as pl
from jax.experimental.pallas import tpu as pltpu
from jax.sharding import PartitionSpec as P

SIDE = 16
PIX = SIDE * SIDE
SLOTS = 256
TILES = 48
CAP = 512
OWNERS = 16
LOCAL = 4096
VIEWS = 8
GROUP = 8
GROUPS = TILES // GROUP
ROWS = GROUP * SLOTS
CHUNK = 256
CHUNK_K = CHUNK // GROUP
CHUNKS = ROWS // CHUNK
SCAT = 512
BLOCK = 512
UNROLL_REDUCE = 4
TOGETHER = 3
UNROLL_GATHER = 4
UNROLL_FORWARD = 4
UNROLL_BACKWARD = 8
UNROLL_SCATTER = 4
UNROLL_SELECT = 4
UNROLL_COLLECT = 4
TURN = 2.0 * math.pi / SIDE
KAPPA = 0.5 / (TURN * TURN)
LOG2E = 1.4426950408889634
DEAD = -1024.0
SEND_ROWS = 48
BACK_ROWS = 56
WIDE = LOCAL + 512 + 128

f32 = jnp.float32
bf16 = jnp.bfloat16

zero_term = 0.28209479177387814
first_term = 0.4886025119029199
second_terms = (
    1.0925484305920792,
    -1.0925484305920792,
    0.31539156525252005,
    -1.0925484305920792,
    0.5462742152960396,
)
third_terms = (
    -0.5900435899266435,
    2.890611442640554,
    -0.4570457994644658,
    0.3731763325901154,
    -0.4570457994644658,
    1.445305721320277,
    -0.5900435899266435,
)
dilation = 0.3


def pixel_tables():
    pixel = np.arange(PIX)
    ang_x = TURN * (pixel % SIDE + 0.5)
    ang_y = TURN * (pixel // SIDE + 0.5)
    sx, cx, sy, cy = np.sin(ang_x), np.cos(ang_x), np.sin(ang_y), np.cos(ang_y)
    rows = np.stack(
        [
            np.ones(PIX),
            np.cos(2 * ang_x),
            np.sin(2 * ang_x),
            np.cos(2 * ang_y),
            np.sin(2 * ang_y),
            sx * sy,
            sx * cy,
            cx * sy,
            cx * cy,
        ]
    )
    kind = ml_dtypes.bfloat16
    parts = []
    rest = rows
    for _ in range(3):
        part = rest.astype(kind)
        parts.append(part)
        rest = rest - part.astype(np.float64)
    order = (0, 1, 2, 0, 1)
    front = np.zeros((128, PIX), kind)
    for at, which in enumerate(order):
        front[8 * at : 8 * at + 8] = parts[which][:8]
        front[40 + at] = parts[which][8]
    back = np.zeros((32, PIX), kind)
    back[0:9] = parts[0]
    back[16:25] = parts[1]
    return front, back


def harmonic_basis(dir_x, dir_y, dir_z):
    square_x = dir_x * dir_x
    square_y = dir_y * dir_y
    square_z = dir_z * dir_z
    return [
        zero_term + 0.0 * dir_x,
        -first_term * dir_y,
        first_term * dir_z,
        -first_term * dir_x,
        second_terms[0] * dir_x * dir_y,
        second_terms[1] * dir_y * dir_z,
        second_terms[2] * (2.0 * square_z - square_x - square_y),
        second_terms[3] * dir_x * dir_z,
        second_terms[4] * (square_x - square_y),
        third_terms[0] * dir_y * (3.0 * square_x - square_y),
        third_terms[1] * dir_x * dir_y * dir_z,
        third_terms[2] * dir_y * (4.0 * square_z - square_x - square_y),
        third_terms[3] * dir_z * (2.0 * square_z - 3.0 * square_x - 3.0 * square_y),
        third_terms[4] * dir_x * (4.0 * square_z - square_x - square_y),
        third_terms[5] * dir_z * (square_x - square_y),
        third_terms[6] * dir_x * (square_x - 3.0 * square_y),
    ]


def iota(shape, axis):
    return lax.broadcasted_iota(jnp.int32, shape, axis)


def wave(cycles):
    part = cycles - jnp.floor(cycles + 0.5)
    x = part * math.pi
    x2 = x * x
    sine = 1.0 / 6227020800.0
    for scale in (-1.0 / 39916800.0, 1.0 / 362880.0, -1.0 / 5040.0, 1.0 / 120.0, -1.0 / 6.0, 1.0):
        sine = sine * x2 + scale
    sine = sine * x
    cosine = -1.0 / 87178291200.0
    for scale in (
        1.0 / 479001600.0,
        -1.0 / 3628800.0,
        1.0 / 40320.0,
        -1.0 / 720.0,
        1.0 / 24.0,
        -0.5,
        1.0,
    ):
        cosine = cosine * x2 + scale
    return 2.0 * sine * cosine, 1.0 - 2.0 * sine * sine


def rotation(rows):
    length = jnp.sqrt(
        rows[0] * rows[0] + rows[1] * rows[1] + rows[2] * rows[2] + rows[3] * rows[3]
    )
    inverse = 1.0 / length
    w, x, y, z = [row * inverse for row in rows]
    matrix = [
        [1.0 - 2.0 * (y * y + z * z), 2.0 * (x * y - w * z), 2.0 * (x * z + w * y)],
        [2.0 * (x * y + w * z), 1.0 - 2.0 * (x * x + z * z), 2.0 * (y * z - w * x)],
        [2.0 * (x * z - w * y), 2.0 * (y * z + w * x), 1.0 - 2.0 * (x * x + y * y)],
    ]
    return inverse, (w, x, y, z), matrix


def halves(value):
    high = value.astype(bf16)
    low = (value - high.astype(f32)).astype(bf16)
    return high, low


def pick(table, lanes):
    return jnp.take_along_axis(table, lanes, axis=1)


def project_kernel(
    angles,
    positions_in,
    log_scales_in,
    rotations_in,
    logit_in,
    sh_in,
    parts,
    aux,
    tab,
    positions,
    log_scales,
    rotations,
    logit,
    sh,
    arrived,
):
    copies = [
        pltpu.make_async_copy(source, place, arrived.at[i])
        for i, (source, place) in enumerate(
            (
                (positions_in, positions),
                (rotations_in, rotations),
                (log_scales_in, log_scales),
                (logit_in, logit),
                (sh_in, sh),
            )
        )
    ]
    for copy in copies:
        copy.start()
    turns = 0.5 / math.pi
    sin_a, cos_a = wave(angles[0:1, 0:1] * turns)
    sin_e, cos_e = wave(angles[0:1, 1:2] * turns)
    right = (-sin_a, cos_a)
    upward = (-sin_e * cos_a, -sin_e * sin_a, cos_e)
    basis = harmonic_basis(cos_e * cos_a, cos_e * sin_a, sin_e)
    for copy in copies:
        copy.wait()
    pos = [positions[i : i + 1, :] for i in range(3)]
    mean_x = right[0] * pos[0] + right[1] * pos[1]
    mean_y = upward[0] * pos[0] + upward[1] * pos[1] + upward[2] * pos[2]
    _, _, matrix = rotation([rotations[i : i + 1, :] for i in range(4)])
    scales = [jnp.exp(log_scales[i : i + 1, :]) for i in range(3)]
    first = [(right[0] * matrix[0][j] + right[1] * matrix[1][j]) * scales[j] for j in range(3)]
    second = [
        (upward[0] * matrix[0][j] + upward[1] * matrix[1][j] + upward[2] * matrix[2][j])
        * scales[j]
        for j in range(3)
    ]
    cov_a = first[0] * first[0] + first[1] * first[1] + first[2] * first[2] + dilation
    cov_b = first[0] * second[0] + first[1] * second[1] + first[2] * second[2]
    cov_c = second[0] * second[0] + second[1] * second[1] + second[2] * second[2] + dilation
    inverse = 1.0 / (cov_a * cov_c - cov_b * cov_b)
    c0, c1, c2 = cov_c * inverse, -cov_b * inverse, cov_a * inverse
    sa, ca = wave(mean_x * (1.0 / SIDE))
    sb, cb = wave(mean_y * (1.0 / SIDE))
    unit = KAPPA * LOG2E
    g0 = -LOG2E * jnp.log(1.0 + jnp.exp(-logit[...])) - (0.5 * unit) * (c0 + c2)
    cross = (-2.0 * unit) * c1
    half_x, half_y = (0.5 * unit) * c0, (0.5 * unit) * c2
    features = [
        g0,
        half_x * (1.0 - 2.0 * sa * sa),
        half_x * (2.0 * sa * ca),
        half_y * (1.0 - 2.0 * sb * sb),
        half_y * (2.0 * sb * cb),
        cross * ca * cb,
        -cross * ca * sb,
        -cross * sa * cb,
        cross * sa * sb,
    ]
    row48 = iota((48, 128), 0)
    weight = jnp.zeros((48, 128), f32)
    for k in range(16):
        weight = jnp.where(row48 // 3 == k, basis[k], weight)
    residue = row48 % 3
    masks = [jnp.where(residue == c, weight, 0.0) for c in range(3)]
    for block in range(LOCAL // 128):
        lanes = slice(128 * block, 128 * block + 128)
        piece = sh[:, lanes]
        for c in range(3):
            raw = 0.5 + jnp.sum(masks[c] * piece, axis=0, keepdims=True)
            aux[7 + c : 8 + c, lanes] = raw
            tab[9 + c : 10 + c, lanes] = jnp.maximum(raw, 0.0)
    for at, row in enumerate(features):
        tab[at : at + 1, :] = row
    for at, row in enumerate((ca, sa, cb, sb, c0, c1, c2)):
        aux[at : at + 1, 0:LOCAL] = row
    aux[10:16, 0:LOCAL] = jnp.zeros((6, LOCAL), f32)
    lane = iota((8, 128), 1)
    sub = iota((8, 128), 0)
    coef = jnp.zeros((8, 128), f32)
    for k in range(16):
        coef = jnp.where((lane // 3 == k) & (sub == 5 + lane % 3), basis[k], coef)

    def put(base, row, at, value):
        return jnp.where((sub == row) & (lane == at), value, base)

    for i in range(3):
        if i < 2:
            coef = put(coef, 0, 48 + i, right[i])
        coef = put(coef, 1, 48 + i, upward[i])
    at = 51
    for i in range(3):
        for j in range(i, 3):
            if j < 2:
                coef = put(coef, 2, at, 2.0 * right[i] * right[j])
            mixed = 0.0
            if i < 2:
                mixed = mixed + right[i] * upward[j]
            if j < 2:
                mixed = mixed + right[j] * upward[i]
            if i < 2 or j < 2:
                coef = put(coef, 3, at, 2.0 * mixed)
            coef = put(coef, 4, at, 2.0 * upward[i] * upward[j])
            at += 1
    aux[0:8, LOCAL : LOCAL + 128] = coef
    aux[8:16, LOCAL : LOCAL + 128] = jnp.zeros((8, 128), f32)

    for h in range(16):
        lanes = slice(256 * h, 256 * h + 256)
        value = tab[0:8, lanes]
        rest = tab[8:12, lanes]
        top = value.astype(bf16).astype(f32)
        peak = rest.astype(bf16).astype(f32)
        stack = jnp.concatenate([top, value - top, peak, rest - peak], axis=0)
        if h % 2 == 0:
            before = stack
        else:
            both = jnp.concatenate([before, stack], axis=0)
            parts[24 * h - 24 : 24 * h + 24, :] = both.astype(bf16)


def unit_rows(spot, width):
    row = iota((16, width), 0).astype(f32)
    one, zero = jnp.ones((16, width), bf16), jnp.zeros((16, width), bf16)
    return jnp.concatenate(
        [jnp.where(spot == (row + 16.0 * s).astype(bf16), one, zero) for s in range(16)], axis=0
    )


def small(ids):
    wide = ids.astype(f32)
    return jnp.concatenate([wide, wide], axis=0).astype(bf16)


def masked_rows(block, count, high, low):
    none = jnp.zeros_like(high)
    tops, lows = [], []
    for h in range(count):
        mask = block == jnp.full(block.shape, h, bf16)
        tops.append(jnp.where(mask, high, none))
        lows.append(jnp.where(mask, low, none))
    return jnp.concatenate(
        [jnp.concatenate(tops, axis=0), jnp.concatenate(lows, axis=0)], axis=1
    )


def select_kernel(wanted, parts, send):
    def one_band(band, carry):
        ids = jnp.concatenate(
            [jnp.broadcast_to(wanted[band, j : j + 1, :], (8, 128)) for j in range(4)], axis=1
        )
        block = lax.shift_right_logical(ids, 8)
        hot = unit_rows(small(ids & 255), CAP)
        found = jnp.dot(parts[...], hot, preferred_element_type=f32)
        acc = [jnp.zeros((8, CAP), f32)] * 3
        for h in range(16):
            mask = block == h
            for part in range(3):
                start = 24 * h + 8 * part
                acc[part] = jnp.where(mask, found[start : start + 8], acc[part])
        value = acc[0] + acc[1]
        rest = acc[2] + pltpu.roll(acc[2], 4, 0)
        for j in range(4):
            lanes = slice(128 * j, 128 * j + 128)
            send[band, 8 * j : 8 * j + 8, :] = value[:, lanes]
            send[band, 32 + 4 * j : 36 + 4 * j, :] = rest[0:4, lanes]
        return carry

    lax.fori_loop(0, OWNERS, one_band, 0, unroll=UNROLL_SELECT)


def blend_kernel(
    table,
    slots,
    order,
    counts,
    target,
    front,
    back,
    images,
    answer,
    tab,
    lhs,
    colours,
    alpha_ref,
    weight_ref,
    high_ref,
    low_ref,
    hot_ref,
    block_ref,
    rise_ref,
    fall_ref,
    grads,
    total,
):
    lane = iota((8, 128), 1)
    sub = iota((8, 128), 0)
    diagonal = sub == (lane & 7)
    diag_wide = iota((8, CHUNK), 0) == (iota((8, CHUNK), 1) & 7)
    depth = lax.shift_right_logical(lane, 3)
    total[...] = jnp.zeros_like(total)
    for owner in range(OWNERS):
        pieces = []
        for part in range(2):
            tops, lows = [], []
            for j in (2 * part, 2 * part + 1):
                value = table[owner, 8 * j : 8 * j + 8, :]
                rest = table[owner, 32 + 4 * j : 36 + 4 * j, :]
                top = value.astype(bf16).astype(f32)
                peak = rest.astype(bf16).astype(f32)
                tops.append(jnp.concatenate([top, value - top, peak, rest - peak], axis=0))
            pieces.append(jnp.concatenate(tops, axis=1))
        tab[48 * owner : 48 * owner + 48, :] = jnp.concatenate(pieces, axis=0).astype(bf16)

    def one_set(index, loss):
        groups = [index * TOGETHER + g for g in range(TOGETHER)]
        starts = [pl.multiple_of(group * GROUP, GROUP) for group in groups]
        limits, ordered = [], []
        for g in range(TOGETHER):
            limits.append(jnp.broadcast_to(counts[pl.ds(groups[g], 1), :], (8, 128)))
            own = slots[pl.ds(starts[g], GROUP), :]
            sequence = order[pl.ds(starts[g], GROUP), :]
            for half in range(2):
                seq = sequence[:, 128 * half : 128 * half + 128]
                spot = seq & 127
                ordered.append(
                    jnp.where(seq < 128, pick(own[:, 0:128], spot), pick(own[:, 128:256], spot))
                )

        def gather(chunk, carry):
            at = pl.multiple_of(chunk * CHUNK, CHUNK)
            for g in range(TOGETHER):
                values = []
                for j in range(2):
                    base = (2 * chunk + j) * 16 + depth
                    value = jnp.where(
                        base < 128,
                        pick(ordered[2 * g], base & 127),
                        pick(ordered[2 * g + 1], base & 127),
                    )
                    value = jnp.sum(jnp.where(diagonal, value, 0), axis=0, keepdims=True)
                    values.append(jnp.broadcast_to(value, (8, 128)))
                ids = jnp.concatenate(values, axis=1)
                block = lax.shift_right_logical(ids, 8)
                hot = unit_rows(small(ids & 255), CHUNK)
                hot_ref[g, :, pl.ds(at, CHUNK)] = hot
                block_ref[g, :, pl.ds(at, CHUNK)] = small(block)
                found = jnp.dot(tab[...], hot, preferred_element_type=f32)
                acc = [jnp.zeros((8, CHUNK), f32)] * 3
                for h in range(32):
                    mask = block == h
                    for part in range(3):
                        start = 24 * h + 8 * part
                        acc[part] = jnp.where(mask, found[start : start + 8], acc[part])
                base = chunk * CHUNK_K + lax.shift_right_logical(iota((8, CHUNK), 1), 3)
                limit = jnp.concatenate([limits[g], limits[g]], axis=1)
                line = iota((8, CHUNK), 0)
                p1 = jnp.where((base >= limit) & (line == 0), DEAD, acc[0])
                p2 = acc[1]

                def spread(which):
                    return jnp.broadcast_to(acc[2][which : which + 1], (8, CHUNK))

                tail = jnp.where(line < 3, spread(0), jnp.where(line < 5, spread(4), 0.0))
                tops = [jnp.where(diag_wide, spread(1 + c), 0.0) for c in range(3)]
                lows = [jnp.where(diag_wide, spread(5 + c), 0.0) for c in range(3)]
                blank = jnp.zeros((8, CHUNK), f32)
                stack = jnp.concatenate(
                    [p1, p1, p1, p2, p2, tail, blank] + tops + tops + lows, axis=0
                )
                lhs[g, pl.ds(at, CHUNK), :] = stack.T.astype(bf16)
                colours[g, :, pl.ds(at, CHUNK)] = jnp.concatenate(tops + lows, axis=0).astype(bf16)
            return carry

        lax.fori_loop(0, CHUNKS, gather, 0, unroll=UNROLL_GATHER)

        def forward(chunk, carry):
            at = pl.multiple_of(chunk * CHUNK, CHUNK)
            result = []
            for g in range(TOGETHER):
                passing, picture = carry[2 * g], carry[2 * g + 1]
                power = jnp.dot(
                    lhs[g, pl.ds(at, CHUNK), :], front[...], preferred_element_type=f32
                )
                alpha = jnp.exp2(power)
                alpha_ref[g, pl.ds(at, CHUNK), :] = alpha
                pieces = []
                for k in range(CHUNK_K):
                    piece = alpha[8 * k : 8 * k + 8] * passing
                    passing = passing - piece
                    pieces.append(piece)
                weight = jnp.concatenate(pieces, axis=0)
                weight_ref[g, pl.ds(at, CHUNK), :] = weight
                high, low = halves(weight)
                high_ref[g, pl.ds(at, CHUNK), :] = high
                low_ref[g, pl.ds(at, CHUNK), :] = low
                own = colours[g, :, pl.ds(at, CHUNK)]
                picture = picture + jnp.dot(own, high, preferred_element_type=f32)
                picture = picture + jnp.dot(own, low, preferred_element_type=f32)
                result += [passing, picture]
            return tuple(result)

        begin = (jnp.ones((8, PIX), f32), jnp.zeros((48, PIX), f32)) * TOGETHER
        done = lax.fori_loop(0, CHUNKS, forward, begin, unroll=UNROLL_FORWARD)
        rights, errs = [], []
        for g in range(TOGETHER):
            picture = done[2 * g + 1]
            picture = picture[0:24] + picture[24:48]
            errors = []
            for c in range(3):
                image = picture[8 * c : 8 * c + 8]
                images[pl.ds(starts[g], GROUP), c, :] = image
                errors.append(image - target[pl.ds(starts[g], GROUP), c, :])
            for error in errors:
                square = error * error
                loss = loss + square[:, 0:128] + square[:, 128:256]
            error = jnp.concatenate(errors, axis=0)
            top = error.astype(bf16).astype(f32)
            bottom = error - top
            right = jnp.concatenate([jnp.zeros((56, PIX), f32), top, bottom, top], axis=0)
            rights.append(right.astype(bf16))
            errs.append(jnp.concatenate([top, bottom], axis=0))

        sides = []
        for g in range(TOGETHER):
            blank = jnp.zeros((96, PIX), f32)
            form = jnp.concatenate([back[...].astype(f32), blank], axis=0).T
            paint = jnp.concatenate([blank[0:32], errs[g], blank[0:48]], axis=0).T
            sides.append(jnp.concatenate([form, form, paint, paint], axis=0).astype(bf16))

        def backward(step, carry):
            at = pl.multiple_of((CHUNKS - 1 - step) * CHUNK, CHUNK)
            result = []
            for g in range(TOGETHER):
                behind = carry[g]
                gain = jnp.dot(
                    lhs[g, pl.ds(at, CHUNK), :], rights[g], preferred_element_type=f32
                )
                alpha = alpha_ref[g, pl.ds(at, CHUNK), :]
                weight = weight_ref[g, pl.ds(at, CHUNK), :]
                pieces = [None] * CHUNK_K
                for k in reversed(range(CHUNK_K)):
                    rows = slice(8 * k, 8 * k + 8)
                    gap = gain[rows] - behind
                    pieces[k] = weight[rows] * gap
                    behind = behind + alpha[rows] * gap
                result.append(behind)
                high, low = halves(jnp.concatenate(pieces, axis=0))
                rise_ref[g, pl.ds(at, CHUNK), :] = high
                fall_ref[g, pl.ds(at, CHUNK), :] = low
            return tuple(result)

        lax.fori_loop(
            0,
            CHUNKS,
            backward,
            (jnp.zeros((8, PIX), f32),) * TOGETHER,
            unroll=UNROLL_BACKWARD,
        )

        def reduce(step, carry):
            at = pl.multiple_of(step * BLOCK, BLOCK)
            row = iota((8, BLOCK), 0)
            match = row == (iota((8, BLOCK), 1) & 7)
            for g in range(TOGETHER):
                pieces = [
                    ref[g, pl.ds(at, BLOCK), :] for ref in (rise_ref, fall_ref, high_ref, low_ref)
                ]
                sums = jnp.dot(
                    jnp.concatenate(pieces, axis=1), sides[g], preferred_element_type=f32
                ).T
                form = sums[0:16] + sums[16:32]
                paint = sums[32:56] + sums[56:80]
                second = form[8:16]
                for c in range(3):
                    own = jnp.where(match, paint[8 * c : 8 * c + 8], 0.0)
                    own = jnp.sum(own, axis=0, keepdims=True)
                    second = jnp.where(row == 1 + c, jnp.broadcast_to(own, (8, BLOCK)), second)
                high, low = halves(jnp.concatenate([form[0:8], second], axis=0))
                grads[g, 0, :, pl.ds(at, BLOCK)] = high
                grads[g, 1, :, pl.ds(at, BLOCK)] = low
            return carry

        lax.fori_loop(0, ROWS // BLOCK, reduce, 0, unroll=UNROLL_REDUCE)

        def scatter(step, carry):
            at = pl.multiple_of(step * SCAT, SCAT)
            for g in range(TOGETHER):
                block = block_ref[g, :, pl.ds(at, SCAT)]
                high = grads[g, 0, :, pl.ds(at, SCAT)]
                low = grads[g, 1, :, pl.ds(at, SCAT)]
                left = masked_rows(block, 32, high, low)
                hot = hot_ref[g, :, pl.ds(at, SCAT)]
                hot = jnp.concatenate([hot, hot], axis=1)
                total[...] += lax.dot_general(
                    left, hot, (((1,), (1,)), ((), ())), preferred_element_type=f32
                )
            return carry

        lax.fori_loop(0, ROWS // SCAT, scatter, 0, unroll=UNROLL_SCATTER)
        return loss

    loss = lax.fori_loop(0, GROUPS // TOGETHER, one_set, jnp.zeros((8, 128), f32))
    for owner in range(OWNERS):
        for j in range(4):
            base = 16 * (2 * owner + j // 2)
            lanes = slice(128 * (j % 2), 128 * (j % 2) + 128)
            answer[owner, 8 * j : 8 * j + 8, :] = total[base : base + 8, lanes]
            answer[owner, 32 + 4 * j : 36 + 4 * j, :] = total[base + 8 : base + 12, lanes]
        answer[owner, 48:56, :] = loss


def blend_scratch():
    return [
        pltpu.VMEM((768, 256), bf16),
        pltpu.VMEM((TOGETHER, ROWS, 128), bf16),
        pltpu.VMEM((TOGETHER, 48, ROWS), bf16),
        pltpu.VMEM((TOGETHER, ROWS, PIX), f32),
        pltpu.VMEM((TOGETHER, ROWS, PIX), f32),
        pltpu.VMEM((TOGETHER, ROWS, PIX), bf16),
        pltpu.VMEM((TOGETHER, ROWS, PIX), bf16),
        pltpu.VMEM((TOGETHER, 256, ROWS), bf16),
        pltpu.VMEM((TOGETHER, 16, ROWS), bf16),
        pltpu.VMEM((TOGETHER, ROWS, PIX), bf16),
        pltpu.VMEM((TOGETHER, ROWS, PIX), bf16),
        pltpu.VMEM((TOGETHER, 2, 16, ROWS), bf16),
        pltpu.VMEM((512, 256), f32),
    ]


def collect_kernel(back, wanted, aux, out, loss, total):
    total[...] = jnp.zeros_like(total)

    def one_band(band, squares):
        tops, lows, blocks, spots = [], [], [], []
        for j in range(4):
            value = jnp.concatenate(
                [
                    back[band, 8 * j : 8 * j + 8, :],
                    back[band, 32 + 4 * j : 36 + 4 * j, :],
                    jnp.zeros((4, 128), f32),
                ],
                axis=0,
            )
            high, low = halves(value)
            tops.append(high)
            lows.append(low)
            ids = jnp.broadcast_to(wanted[band, j : j + 1, :], (8, 128))
            blocks.append(lax.shift_right_logical(ids, 8))
            spots.append(ids & 255)
        high = jnp.concatenate(tops, axis=1)
        low = jnp.concatenate(lows, axis=1)
        block = jnp.concatenate(blocks, axis=1)
        spot = jnp.concatenate(spots, axis=1)
        left = masked_rows(small(block), 16, high, low)
        hot = unit_rows(small(spot), CAP)
        hot = jnp.concatenate([hot, hot], axis=1)
        total[...] += lax.dot_general(
            left, hot, (((1,), (1,)), ((), ())), preferred_element_type=f32
        )
        return squares + back[band, 48:56, :]

    squares = lax.fori_loop(
        0, OWNERS, one_band, jnp.zeros((8, 128), f32), unroll=UNROLL_COLLECT
    )
    whole = jnp.sum(jnp.sum(squares, axis=1, keepdims=True), axis=0, keepdims=True)
    loss[...] = whole * (1.0 / (TILES * OWNERS * PIX * 3))
    for h in range(16):
        lanes = slice(256 * h, 256 * h + 256)
        gain = [total[16 * h + c : 16 * h + c + 1, :] for c in range(12)]
        ca, sa, cb, sb, c0, c1, c2 = [aux[c : c + 1, lanes] for c in range(7)]
        cos_x, sin_x = 1.0 - 2.0 * sa * sa, 2.0 * sa * ca
        cos_y, sin_y = 1.0 - 2.0 * sb * sb, 2.0 * sb * cb
        d0 = (0.5 * KAPPA) * (cos_x * gain[1] + sin_x * gain[2] - gain[0])
        d2 = (0.5 * KAPPA) * (cos_y * gain[3] + sin_y * gain[4] - gain[0])
        cacb, casb, sacb, sasb = ca * cb, ca * sb, sa * cb, sa * sb
        d1 = (2.0 * KAPPA) * (casb * gain[6] - cacb * gain[5] + sacb * gain[7] - sasb * gain[8])
        twist = (2.0 * KAPPA) * c1
        da = KAPPA * c0 * (cos_x * gain[2] - sin_x * gain[1]) + twist * (
            sacb * gain[5] - sasb * gain[6] + cacb * gain[7] - casb * gain[8]
        )
        db = KAPPA * c2 * (cos_y * gain[4] - sin_y * gain[3]) + twist * (
            casb * gain[5] + cacb * gain[6] - sasb * gain[7] - sacb * gain[8]
        )
        out[0:1, lanes] = TURN * da
        out[1:2, lanes] = TURN * db
        out[2:3, lanes] = -(c0 * c0 * d0 + c0 * c1 * d1 + c1 * c1 * d2)
        out[3:4, lanes] = -(c0 * c1 * d0 + 0.5 * (c0 * c2 + c1 * c1) * d1 + c1 * c2 * d2)
        out[4:5, lanes] = -(c1 * c1 * d0 + c1 * c2 * d1 + c2 * c2 * d2)
        for c in range(3):
            raw = aux[7 + c : 8 + c, lanes]
            share = jnp.where(raw > 0.0, 1.0, jnp.where(raw == 0.0, 0.5, 0.0))
            out[5 + c : 6 + c, lanes] = share * gain[9 + c]
        spot = LOCAL + 256 * (h % 2)
        out[h // 2 : h // 2 + 1, spot : spot + 256] = gain[0]
    out[:, LOCAL + 512 :] = aux[0:8, LOCAL : LOCAL + 128]


def finish_kernel(
    near, far, log_scales, rotations, logit, grad_pos, grad_log, grad_rot, grad_op, grad_sh, work
):
    gathered = [ref.at[i] for ref in (near, far) for i in range(VIEWS // 2)]
    coef = jnp.concatenate([gathered[view][:, LOCAL + 512 :] for view in range(VIEWS)], axis=0)
    high, low = halves(coef.T)
    left = jnp.concatenate([high, low, high], axis=1)[0:64]
    for block in range(LOCAL // 512):
        lanes = slice(512 * block, 512 * block + 512)
        value = jnp.concatenate([gathered[view][:, lanes] for view in range(VIEWS)], axis=0)
        top, bottom = halves(value)
        right = jnp.concatenate([top, top, bottom], axis=0)
        work[:, lanes] = jnp.dot(left, right, preferred_element_type=f32)
    grad_sh[...] = work[0:48, :]
    grad_pos[...] = work[48:51, :]
    shade = gathered[0][:, LOCAL : LOCAL + 512]
    for view in range(1, VIEWS):
        shade = shade + gathered[view][:, LOCAL : LOCAL + 512]
    shade = jnp.concatenate([shade[s : s + 1, :] for s in range(8)], axis=1)
    grad_op[...] = shade / (1.0 + jnp.exp(logit[...]))
    k00, k01, k02, k11, k12, k22 = [work[51 + i : 52 + i, :] for i in range(6)]
    spread = [[k00, k01, k02], [k01, k11, k12], [k02, k12, k22]]
    inverse, (w, x, y, z), matrix = rotation([rotations[i : i + 1, :] for i in range(4)])
    d = [[None] * 3 for _ in range(3)]
    for j in range(3):
        scale = jnp.exp(log_scales[j : j + 1, :])
        square = scale * scale
        grad = None
        for i in range(3):
            value = (
                spread[i][0] * matrix[0][j]
                + spread[i][1] * matrix[1][j]
                + spread[i][2] * matrix[2][j]
            ) * square
            d[i][j] = value
            term = value * matrix[i][j]
            grad = term if grad is None else grad + term
        grad_log[j : j + 1, :] = grad
    dw = 2.0 * (x * (d[2][1] - d[1][2]) + y * (d[0][2] - d[2][0]) + z * (d[1][0] - d[0][1]))
    dx = 2.0 * (
        y * (d[0][1] + d[1][0])
        + z * (d[0][2] + d[2][0])
        + w * (d[2][1] - d[1][2])
        - 2.0 * x * (d[1][1] + d[2][2])
    )
    dy = 2.0 * (
        x * (d[0][1] + d[1][0])
        + z * (d[1][2] + d[2][1])
        + w * (d[0][2] - d[2][0])
        - 2.0 * y * (d[0][0] + d[2][2])
    )
    dz = 2.0 * (
        x * (d[0][2] + d[2][0])
        + y * (d[1][2] + d[2][1])
        + w * (d[1][0] - d[0][1])
        - 2.0 * z * (d[0][0] + d[1][1])
    )
    along = w * dw + x * dx + y * dy + z * dz
    for at, (part, unit) in enumerate(((dw, w), (dx, x), (dy, y), (dz, z))):
        grad_rot[at : at + 1, :] = (part - unit * along) * inverse


def whole():
    return pl.BlockSpec(memory_space=pltpu.VMEM)


def params(mega):
    return pltpu.CompilerParams(vmem_limit_bytes=mega << 20)


def shape(*dims):
    return jax.ShapeDtypeStruct(dims, f32)


def local(
    positions,
    log_scales,
    rotations,
    opacity_logit,
    sh_coeffs,
    view_angles,
    target,
    fetch_index,
    tile_slots,
    depth_order,
    block_count,
):
    wanted = lax.all_to_all(
        fetch_index.reshape(OWNERS, 4, 128), "band", split_axis=0, concat_axis=0, tiled=True
    )
    counts = jnp.tile(block_count.reshape(GROUPS, GROUP), (1, 16))
    front, back = pixel_tables()
    parts, aux = pl.pallas_call(
        project_kernel,
        out_shape=(jax.ShapeDtypeStruct((384, 256), bf16), shape(16, LOCAL + 128)),
        in_specs=[whole()] + [pl.BlockSpec(memory_space=pl.ANY)] * 5,
        out_specs=(whole(), whole()),
        scratch_shapes=[pltpu.VMEM((rows, LOCAL), f32) for rows in (16, 3, 3, 4, 1, 48)]
        + [pltpu.SemaphoreType.DMA((5,))],
        compiler_params=params(56),
        name="project",
    )(view_angles, positions, log_scales, rotations, opacity_logit, sh_coeffs)
    send = pl.pallas_call(
        select_kernel,
        out_shape=shape(OWNERS, SEND_ROWS, 128),
        in_specs=[whole()] * 2,
        out_specs=whole(),
        compiler_params=params(32),
        name="select",
    )(wanted, parts)
    table = lax.all_to_all(send, "band", split_axis=0, concat_axis=0, tiled=True)
    images, answer = pl.pallas_call(
        blend_kernel,
        out_shape=(shape(TILES, 3, PIX), shape(OWNERS, BACK_ROWS, 128)),
        in_specs=[whole()] * 7,
        out_specs=(whole(), whole()),
        scratch_shapes=blend_scratch(),
        compiler_params=params(42),
        name="blend",
    )(
        table,
        tile_slots[0],
        depth_order[0],
        counts,
        target[0],
        jnp.asarray(front),
        jnp.asarray(back),
    )
    returned = lax.all_to_all(answer, "band", split_axis=0, concat_axis=0, tiled=True)
    share, loss = pl.pallas_call(
        collect_kernel,
        out_shape=(shape(8, WIDE), shape(1, 1)),
        in_specs=[whole()] * 3,
        out_specs=(whole(), whole()),
        scratch_shapes=[pltpu.VMEM((256, 256), f32)],
        compiler_params=params(32),
        name="collect",
    )(returned, wanted, aux)
    around = [share]
    for step in (4, 2, 6):
        ring = [(v, (v + step) % VIEWS) for v in range(VIEWS)]
        around.append(lax.ppermute(share, "view", ring))
    near = jnp.stack(around)
    far = lax.ppermute(near, "view", [(v, v ^ 1) for v in range(VIEWS)])
    grads = pl.pallas_call(
        finish_kernel,
        out_shape=(
            shape(3, LOCAL),
            shape(3, LOCAL),
            shape(4, LOCAL),
            shape(1, LOCAL),
            shape(48, LOCAL),
        ),
        in_specs=[whole()] * 5,
        out_specs=(whole(),) * 5,
        scratch_shapes=[pltpu.VMEM((64, LOCAL), f32)],
        compiler_params=params(32),
        name="finish",
    )(near, far, log_scales, rotations, opacity_logit)
    return (images[None], loss.reshape(1)) + tuple(grads)


def solution(mesh):
    in_specs = (
        P(None, "band"),
        P(None, "band"),
        P(None, "band"),
        P(None, "band"),
        P(None, "band"),
        P("view", None),
        P("view", "band", None, None),
        P("view", "band", None, None),
        P("view", "band", None),
        P("view", "band", None),
        P("view", "band"),
    )
    out_specs = (
        P("view", "band", None, None),
        P("view"),
        P(None, "band"),
        P(None, "band"),
        P(None, "band"),
        P(None, "band"),
        P(None, "band"),
    )
    return jax.shard_map(local, mesh=mesh, in_specs=in_specs, out_specs=out_specs, check_vma=False)
```

```python
import math

import jax
import jax.numpy as jnp
import ml_dtypes
import numpy as np
from jax import lax
from jax.experimental import pallas as pl
from jax.experimental.pallas import tpu as pltpu
from jax.sharding import PartitionSpec as P

SIDE = 16
PIX = SIDE * SIDE
SLOTS = 256
TILES = 48
CAP = 512
OWNERS = 16
LOCAL = 4096
VIEWS = 8
GROUP = 8
GROUPS = TILES // GROUP
ROWS = GROUP * SLOTS
CHUNK = 256
CHUNK_K = CHUNK // GROUP
CHUNKS = ROWS // CHUNK
SCAT = 512
BLOCK = 512
UNROLL_REDUCE = 4
TOGETHER = 3
UNROLL_GATHER = 4
UNROLL_FORWARD = 8
UNROLL_BACKWARD = 8
UNROLL_SCATTER = 4
UNROLL_SELECT = 4
UNROLL_COLLECT = 4
TURN = 2.0 * math.pi / SIDE
KAPPA = 0.5 / (TURN * TURN)
LOG2E = 1.4426950408889634
DEAD = -1024.0
SEND_ROWS = 48
BACK_ROWS = 56
WIDE = LOCAL + 512 + 128

f32 = jnp.float32
bf16 = jnp.bfloat16

zero_term = 0.28209479177387814
first_term = 0.4886025119029199
second_terms = (
    1.0925484305920792,
    -1.0925484305920792,
    0.31539156525252005,
    -1.0925484305920792,
    0.5462742152960396,
)
third_terms = (
    -0.5900435899266435,
    2.890611442640554,
    -0.4570457994644658,
    0.3731763325901154,
    -0.4570457994644658,
    1.445305721320277,
    -0.5900435899266435,
)
dilation = 0.3


def pixel_tables():
    pixel = np.arange(PIX)
    ang_x = TURN * (pixel % SIDE + 0.5)
    ang_y = TURN * (pixel // SIDE + 0.5)
    sx, cx, sy, cy = np.sin(ang_x), np.cos(ang_x), np.sin(ang_y), np.cos(ang_y)
    rows = np.stack(
        [
            np.ones(PIX),
            np.cos(2 * ang_x),
            np.sin(2 * ang_x),
            np.cos(2 * ang_y),
            np.sin(2 * ang_y),
            sx * sy,
            sx * cy,
            cx * sy,
            cx * cy,
        ]
    )
    kind = ml_dtypes.bfloat16
    parts = []
    rest = rows
    for _ in range(3):
        part = rest.astype(kind)
        parts.append(part)
        rest = rest - part.astype(np.float64)
    order = (0, 1, 2, 0, 1)
    front = np.zeros((128, PIX), kind)
    for at, which in enumerate(order):
        front[8 * at : 8 * at + 8] = parts[which][:8]
        front[40 + at] = parts[which][8]
    early = pixel % SIDE < SIDE // 2
    kept = np.where(np.arange(9)[:, None] < 5, early, ~early)
    back = np.zeros((32, PIX), kind)
    for at in (0, PIX // 2):
        half = slice(at, at + PIX // 2)
        back[0:9, half] = np.where(kept, parts[0], 0)[:, : PIX // 2]
        back[16:25, half] = np.where(kept, parts[1], 0)[:, : PIX // 2]
    return front, back


def harmonic_basis(dir_x, dir_y, dir_z):
    square_x = dir_x * dir_x
    square_y = dir_y * dir_y
    square_z = dir_z * dir_z
    return [
        zero_term + 0.0 * dir_x,
        -first_term * dir_y,
        first_term * dir_z,
        -first_term * dir_x,
        second_terms[0] * dir_x * dir_y,
        second_terms[1] * dir_y * dir_z,
        second_terms[2] * (2.0 * square_z - square_x - square_y),
        second_terms[3] * dir_x * dir_z,
        second_terms[4] * (square_x - square_y),
        third_terms[0] * dir_y * (3.0 * square_x - square_y),
        third_terms[1] * dir_x * dir_y * dir_z,
        third_terms[2] * dir_y * (4.0 * square_z - square_x - square_y),
        third_terms[3] * dir_z * (2.0 * square_z - 3.0 * square_x - 3.0 * square_y),
        third_terms[4] * dir_x * (4.0 * square_z - square_x - square_y),
        third_terms[5] * dir_z * (square_x - square_y),
        third_terms[6] * dir_x * (square_x - 3.0 * square_y),
    ]


def iota(shape, axis):
    return lax.broadcasted_iota(jnp.int32, shape, axis)


def wave(cycles):
    part = cycles - jnp.floor(cycles + 0.5)
    x = part * math.pi
    x2 = x * x
    sine = 1.0 / 6227020800.0
    for scale in (-1.0 / 39916800.0, 1.0 / 362880.0, -1.0 / 5040.0, 1.0 / 120.0, -1.0 / 6.0, 1.0):
        sine = sine * x2 + scale
    sine = sine * x
    cosine = -1.0 / 87178291200.0
    for scale in (
        1.0 / 479001600.0,
        -1.0 / 3628800.0,
        1.0 / 40320.0,
        -1.0 / 720.0,
        1.0 / 24.0,
        -0.5,
        1.0,
    ):
        cosine = cosine * x2 + scale
    return 2.0 * sine * cosine, 1.0 - 2.0 * sine * sine


def rotation(rows):
    length = jnp.sqrt(
        rows[0] * rows[0] + rows[1] * rows[1] + rows[2] * rows[2] + rows[3] * rows[3]
    )
    inverse = 1.0 / length
    w, x, y, z = [row * inverse for row in rows]
    matrix = [
        [1.0 - 2.0 * (y * y + z * z), 2.0 * (x * y - w * z), 2.0 * (x * z + w * y)],
        [2.0 * (x * y + w * z), 1.0 - 2.0 * (x * x + z * z), 2.0 * (y * z - w * x)],
        [2.0 * (x * z - w * y), 2.0 * (y * z + w * x), 1.0 - 2.0 * (x * x + y * y)],
    ]
    return inverse, (w, x, y, z), matrix


def halves(value):
    high = value.astype(bf16)
    low = (value - high.astype(f32)).astype(bf16)
    return high, low


def pick(table, lanes):
    return jnp.take_along_axis(table, lanes, axis=1)


def project_kernel(angles, positions, log_scales, rotations, logit, sh, parts, aux, tab):
    turns = 0.5 / math.pi
    sin_a, cos_a = wave(angles[0:1, 0:1] * turns)
    sin_e, cos_e = wave(angles[0:1, 1:2] * turns)
    right = (-sin_a, cos_a)
    upward = (-sin_e * cos_a, -sin_e * sin_a, cos_e)
    basis = harmonic_basis(cos_e * cos_a, cos_e * sin_a, sin_e)
    pos = [positions[i : i + 1, :] for i in range(3)]
    mean_x = right[0] * pos[0] + right[1] * pos[1]
    mean_y = upward[0] * pos[0] + upward[1] * pos[1] + upward[2] * pos[2]
    _, _, matrix = rotation([rotations[i : i + 1, :] for i in range(4)])
    scales = [jnp.exp(log_scales[i : i + 1, :]) for i in range(3)]
    first = [(right[0] * matrix[0][j] + right[1] * matrix[1][j]) * scales[j] for j in range(3)]
    second = [
        (upward[0] * matrix[0][j] + upward[1] * matrix[1][j] + upward[2] * matrix[2][j])
        * scales[j]
        for j in range(3)
    ]
    cov_a = first[0] * first[0] + first[1] * first[1] + first[2] * first[2] + dilation
    cov_b = first[0] * second[0] + first[1] * second[1] + first[2] * second[2]
    cov_c = second[0] * second[0] + second[1] * second[1] + second[2] * second[2] + dilation
    inverse = 1.0 / (cov_a * cov_c - cov_b * cov_b)
    c0, c1, c2 = cov_c * inverse, -cov_b * inverse, cov_a * inverse
    sa, ca = wave(mean_x * (1.0 / SIDE))
    sb, cb = wave(mean_y * (1.0 / SIDE))
    unit = KAPPA * LOG2E
    g0 = -LOG2E * jnp.log(1.0 + jnp.exp(-logit[...])) - (0.5 * unit) * (c0 + c2)
    cross = (-2.0 * unit) * c1
    half_x, half_y = (0.5 * unit) * c0, (0.5 * unit) * c2
    features = [
        g0,
        half_x * (1.0 - 2.0 * sa * sa),
        half_x * (2.0 * sa * ca),
        half_y * (1.0 - 2.0 * sb * sb),
        half_y * (2.0 * sb * cb),
        cross * ca * cb,
        -cross * ca * sb,
        -cross * sa * cb,
        cross * sa * sb,
    ]
    row48 = iota((48, 128), 0)
    weight = jnp.zeros((48, 128), f32)
    for k in range(16):
        weight = jnp.where(row48 // 3 == k, basis[k], weight)
    residue = row48 % 3
    masks = [jnp.where(residue == c, weight, 0.0) for c in range(3)]
    for block in range(LOCAL // 128):
        lanes = slice(128 * block, 128 * block + 128)
        piece = sh[:, lanes]
        for c in range(3):
            raw = 0.5 + jnp.sum(masks[c] * piece, axis=0, keepdims=True)
            aux[7 + c : 8 + c, lanes] = raw
            tab[9 + c : 10 + c, lanes] = jnp.maximum(raw, 0.0)
    for at, row in enumerate(features):
        tab[at : at + 1, :] = row
    for at, row in enumerate((ca, sa, cb, sb, c0, c1, c2)):
        aux[at : at + 1, 0:LOCAL] = row
    aux[10:16, 0:LOCAL] = jnp.zeros((6, LOCAL), f32)
    lane = iota((8, 128), 1)
    sub = iota((8, 128), 0)
    coef = jnp.zeros((8, 128), f32)
    for k in range(16):
        coef = jnp.where((lane // 3 == k) & (sub == 5 + lane % 3), basis[k], coef)

    def put(base, row, at, value):
        return jnp.where((sub == row) & (lane == at), value, base)

    for i in range(3):
        if i < 2:
            coef = put(coef, 0, 48 + i, right[i])
        coef = put(coef, 1, 48 + i, upward[i])
    at = 51
    for i in range(3):
        for j in range(i, 3):
            if j < 2:
                coef = put(coef, 2, at, 2.0 * right[i] * right[j])
            mixed = 0.0
            if i < 2:
                mixed = mixed + right[i] * upward[j]
            if j < 2:
                mixed = mixed + right[j] * upward[i]
            if i < 2 or j < 2:
                coef = put(coef, 3, at, 2.0 * mixed)
            coef = put(coef, 4, at, 2.0 * upward[i] * upward[j])
            at += 1
    aux[0:8, LOCAL : LOCAL + 128] = coef
    aux[8:16, LOCAL : LOCAL + 128] = jnp.zeros((8, 128), f32)

    for h in range(16):
        lanes = slice(256 * h, 256 * h + 256)
        value = tab[0:8, lanes]
        rest = tab[8:12, lanes]
        top = value.astype(bf16).astype(f32)
        peak = rest.astype(bf16).astype(f32)
        stack = jnp.concatenate([top, value - top, peak, rest - peak], axis=0)
        if h % 2 == 0:
            before = stack
        else:
            both = jnp.concatenate([before, stack], axis=0)
            parts[24 * h - 24 : 24 * h + 24, :] = both.astype(bf16)


def unit_rows(spot, width):
    row = iota((16, width), 0).astype(f32)
    one, zero = jnp.ones((16, width), bf16), jnp.zeros((16, width), bf16)
    return jnp.concatenate(
        [jnp.where(spot == (row + 16.0 * s).astype(bf16), one, zero) for s in range(16)], axis=0
    )


def small(ids):
    wide = ids.astype(f32)
    return jnp.concatenate([wide, wide], axis=0).astype(bf16)


def masked_rows(block, count, high, low):
    width = block.shape[1]
    row = iota((16, width), 0)
    by_eight = lax.shift_right_logical(row, 3).astype(f32)
    by_four = lax.shift_right_logical(row, 2).astype(f32)
    none = jnp.zeros((16, width), bf16)
    shares = []
    for value in (high, low):
        wide = value.astype(f32)
        head, tail = wide[0:8], wide[8:12]
        shares.append(
            (
                jnp.concatenate([head, head], axis=0).astype(bf16),
                jnp.concatenate([tail, tail, tail, tail], axis=0).astype(bf16),
            )
        )
    sets = ([], [])
    for h in range(0, count, 4):
        masks = [
            block == (by_eight + h).astype(bf16),
            block == (by_eight + (h + 2.0)).astype(bf16),
            block == (by_four + h).astype(bf16),
        ]
        for rows, (head, tail) in zip(sets, shares):
            rows.append(jnp.where(masks[0], head, none))
            rows.append(jnp.where(masks[1], head, none))
            rows.append(jnp.where(masks[2], tail, none))
    return jnp.concatenate(sets[0] + sets[1], axis=0)


def place_of(block):
    base = 48 * (block // 4)
    return base + 8 * (block % 4), base + 32 + 4 * (block % 4)


def add_products(total, left, hot):
    both = lax.dot_general(left, hot, (((1,), (1,)), ((), ())), preferred_element_type=f32)
    half = both.shape[0] // 2
    total[...] += both[0:half] + both[half:]


def select_kernel(wanted, parts, send):
    def one_band(band, carry):
        ids = jnp.concatenate(
            [jnp.broadcast_to(wanted[band, j : j + 1, :], (8, 128)) for j in range(4)], axis=1
        )
        block = lax.shift_right_logical(ids, 8)
        hot = unit_rows(small(ids & 255), CAP)
        found = jnp.dot(parts[...], hot, preferred_element_type=f32)
        acc = [jnp.zeros((8, CAP), f32)] * 3
        for h in range(16):
            mask = block == h
            for part in range(3):
                start = 24 * h + 8 * part
                acc[part] = jnp.where(mask, found[start : start + 8], acc[part])
        value = acc[0] + acc[1]
        rest = acc[2] + pltpu.roll(acc[2], 4, 0)
        for j in range(4):
            lanes = slice(128 * j, 128 * j + 128)
            send[band, 8 * j : 8 * j + 8, :] = value[:, lanes]
            send[band, 32 + 4 * j : 36 + 4 * j, :] = rest[0:4, lanes]
        return carry

    lax.fori_loop(0, OWNERS, one_band, 0, unroll=UNROLL_SELECT)


def blend_kernel(
    table,
    slots,
    order,
    counts,
    target,
    front,
    back,
    images,
    answer,
    tab,
    lhs,
    colours,
    alpha_ref,
    weight_ref,
    high_ref,
    low_ref,
    hot_ref,
    block_ref,
    fold_ref,
    grads,
    total,
):
    lane = iota((8, 128), 1)
    sub = iota((8, 128), 0)
    diagonal = sub == (lane & 7)
    diag_wide = iota((8, CHUNK), 0) == (iota((8, CHUNK), 1) & 7)
    depth = lax.shift_right_logical(lane, 3)
    early = (iota((CHUNK, 128), 1) & (SIDE - 1)) < SIDE // 2
    total[...] = jnp.zeros_like(total)
    for owner in range(OWNERS):
        pieces = []
        for part in range(2):
            tops, lows = [], []
            for j in (2 * part, 2 * part + 1):
                value = table[owner, 8 * j : 8 * j + 8, :]
                rest = table[owner, 32 + 4 * j : 36 + 4 * j, :]
                top = value.astype(bf16).astype(f32)
                peak = rest.astype(bf16).astype(f32)
                tops.append(jnp.concatenate([top, value - top, peak, rest - peak], axis=0))
            pieces.append(jnp.concatenate(tops, axis=1))
        tab[48 * owner : 48 * owner + 48, :] = jnp.concatenate(pieces, axis=0).astype(bf16)

    def one_set(index, loss):
        groups = [index * TOGETHER + g for g in range(TOGETHER)]
        starts = [pl.multiple_of(group * GROUP, GROUP) for group in groups]
        limits, ordered = [], []
        for g in range(TOGETHER):
            limits.append(jnp.broadcast_to(counts[pl.ds(groups[g], 1), :], (8, 128)))
            own = slots[pl.ds(starts[g], GROUP), :]
            sequence = order[pl.ds(starts[g], GROUP), :]
            for half in range(2):
                seq = sequence[:, 128 * half : 128 * half + 128]
                spot = seq & 127
                ordered.append(
                    jnp.where(seq < 128, pick(own[:, 0:128], spot), pick(own[:, 128:256], spot))
                )

        def gather(chunk, carry):
            at = pl.multiple_of(chunk * CHUNK, CHUNK)
            for g in range(TOGETHER):
                values = []
                for j in range(2):
                    base = (2 * chunk + j) * 16 + depth
                    value = jnp.where(
                        base < 128,
                        pick(ordered[2 * g], base & 127),
                        pick(ordered[2 * g + 1], base & 127),
                    )
                    value = jnp.sum(jnp.where(diagonal, value, 0), axis=0, keepdims=True)
                    values.append(jnp.broadcast_to(value, (8, 128)))
                ids = jnp.concatenate(values, axis=1)
                block = lax.shift_right_logical(ids, 8)
                hot = unit_rows(small(ids & 255), CHUNK)
                hot_ref[g, :, pl.ds(at, CHUNK)] = hot
                block_ref[g, :, pl.ds(at, CHUNK)] = small(block)
                found = jnp.dot(tab[...], hot, preferred_element_type=f32)
                acc = [jnp.zeros((8, CHUNK), f32)] * 3
                for h in range(32):
                    mask = block == h
                    for part in range(3):
                        start = 24 * h + 8 * part
                        acc[part] = jnp.where(mask, found[start : start + 8], acc[part])
                base = chunk * CHUNK_K + lax.shift_right_logical(iota((8, CHUNK), 1), 3)
                limit = jnp.concatenate([limits[g], limits[g]], axis=1)
                line = iota((8, CHUNK), 0)
                p1 = jnp.where((base >= limit) & (line == 0), DEAD, acc[0])
                p2 = acc[1]

                def spread(which):
                    return jnp.broadcast_to(acc[2][which : which + 1], (8, CHUNK))

                tail = jnp.where(line < 3, spread(0), jnp.where(line < 5, spread(4), 0.0))
                tops = [jnp.where(diag_wide, spread(1 + c), 0.0) for c in range(3)]
                lows = [jnp.where(diag_wide, spread(5 + c), 0.0) for c in range(3)]
                blank = jnp.zeros((8, CHUNK), f32)
                stack = jnp.concatenate(
                    [p1, p1, p1, p2, p2, tail, blank] + tops + tops + lows, axis=0
                )
                lhs[g, pl.ds(at, CHUNK), :] = stack.T.astype(bf16)
                colours[g, :, pl.ds(at, CHUNK)] = jnp.concatenate(tops + lows, axis=0).astype(bf16)
            return carry

        lax.fori_loop(0, CHUNKS, gather, 0, unroll=UNROLL_GATHER)

        def forward(chunk, carry):
            at = pl.multiple_of(chunk * CHUNK, CHUNK)
            result = []
            for g in range(TOGETHER):
                passing, picture = carry[2 * g], carry[2 * g + 1]
                power = jnp.dot(
                    lhs[g, pl.ds(at, CHUNK), :], front[...], preferred_element_type=f32
                )
                alpha = jnp.exp2(power)
                alpha_ref[g, pl.ds(at, CHUNK), :] = alpha
                pieces = []
                for k in range(CHUNK_K):
                    piece = alpha[8 * k : 8 * k + 8] * passing
                    passing = passing - piece
                    pieces.append(piece)
                weight = jnp.concatenate(pieces, axis=0)
                weight_ref[g, pl.ds(at, CHUNK), :] = weight
                high, low = halves(weight)
                high_ref[g, pl.ds(at, CHUNK), :] = high
                low_ref[g, pl.ds(at, CHUNK), :] = low
                own = colours[g, :, pl.ds(at, CHUNK)]
                picture = picture + jnp.dot(own, high, preferred_element_type=f32)
                picture = picture + jnp.dot(own, low, preferred_element_type=f32)
                result += [passing, picture]
            return tuple(result)

        begin = (jnp.ones((8, PIX), f32), jnp.zeros((48, PIX), f32)) * TOGETHER
        done = lax.fori_loop(0, CHUNKS, forward, begin, unroll=UNROLL_FORWARD)
        rights, errs = [], []
        for g in range(TOGETHER):
            picture = done[2 * g + 1]
            picture = picture[0:24] + picture[24:48]
            errors = []
            for c in range(3):
                image = picture[8 * c : 8 * c + 8]
                images[pl.ds(starts[g], GROUP), c, :] = image
                errors.append(image - target[pl.ds(starts[g], GROUP), c, :])
            for error in errors:
                square = error * error
                loss = loss + square[:, 0:128] + square[:, 128:256]
            error = jnp.concatenate(errors, axis=0)
            top = error.astype(bf16).astype(f32)
            bottom = error - top
            right = jnp.concatenate([jnp.zeros((56, PIX), f32), top, bottom, top], axis=0)
            rights.append(right.astype(bf16))
            errs.append(jnp.concatenate([top, bottom], axis=0))

        sides = []
        for g in range(TOGETHER):
            blank = jnp.zeros((96, PIX), f32)
            form = jnp.concatenate([back[...].astype(f32), blank], axis=0).T
            paint = jnp.concatenate([blank[0:32], errs[g], blank[0:48]], axis=0).T
            sides.append(jnp.concatenate([form, paint, paint], axis=0).astype(bf16))

        def backward(step, carry):
            at = pl.multiple_of((CHUNKS - 1 - step) * CHUNK, CHUNK)
            result = []
            for g in range(TOGETHER):
                behind = carry[g]
                gain = jnp.dot(
                    lhs[g, pl.ds(at, CHUNK), :], rights[g], preferred_element_type=f32
                )
                alpha = alpha_ref[g, pl.ds(at, CHUNK), :]
                weight = weight_ref[g, pl.ds(at, CHUNK), :]
                pieces = [None] * CHUNK_K
                for k in reversed(range(CHUNK_K)):
                    rows = slice(8 * k, 8 * k + 8)
                    gap = gain[rows] - behind
                    pieces[k] = weight[rows] * gap
                    behind = behind + alpha[rows] * gap
                result.append(behind)
                whole_rows = jnp.concatenate(pieces, axis=0)
                upper, lower = whole_rows[:, 0:128], whole_rows[:, 128:256]
                even, odd = upper + lower, upper - lower
                folded = jnp.where(
                    early, even + pltpu.roll(even, 120, 1), odd - pltpu.roll(odd, 8, 1)
                )
                fold_ref[g, pl.ds(at, CHUNK), :] = jnp.concatenate(halves(folded), axis=1)
            return tuple(result)

        lax.fori_loop(
            0,
            CHUNKS,
            backward,
            (jnp.zeros((8, PIX), f32),) * TOGETHER,
            unroll=UNROLL_BACKWARD,
        )

        def reduce(step, carry):
            at = pl.multiple_of(step * BLOCK, BLOCK)
            row = iota((8, BLOCK), 0)
            match = row == (iota((8, BLOCK), 1) & 7)
            for g in range(TOGETHER):
                pieces = [ref[g, pl.ds(at, BLOCK), :] for ref in (fold_ref, high_ref, low_ref)]
                sums = jnp.dot(
                    jnp.concatenate(pieces, axis=1), sides[g], preferred_element_type=f32
                ).T
                form = sums[0:16] + sums[16:32]
                paint = sums[32:56] + sums[56:80]
                second = form[8:16]
                for c in range(3):
                    own = jnp.where(match, paint[8 * c : 8 * c + 8], 0.0)
                    own = jnp.sum(own, axis=0, keepdims=True)
                    second = jnp.where(row == 1 + c, jnp.broadcast_to(own, (8, BLOCK)), second)
                high, low = halves(jnp.concatenate([form[0:8], second], axis=0))
                grads[g, 0, :, pl.ds(at, BLOCK)] = high
                grads[g, 1, :, pl.ds(at, BLOCK)] = low
            return carry

        lax.fori_loop(0, ROWS // BLOCK, reduce, 0, unroll=UNROLL_REDUCE)

        def scatter(step, carry):
            at = pl.multiple_of(step * SCAT, SCAT)
            for g in range(TOGETHER):
                block = block_ref[g, :, pl.ds(at, SCAT)]
                high = grads[g, 0, :, pl.ds(at, SCAT)]
                low = grads[g, 1, :, pl.ds(at, SCAT)]
                left = masked_rows(block, 32, high, low)
                add_products(total, left, hot_ref[g, :, pl.ds(at, SCAT)])
            return carry

        lax.fori_loop(0, ROWS // SCAT, scatter, 0, unroll=UNROLL_SCATTER)
        return loss

    loss = lax.fori_loop(0, GROUPS // TOGETHER, one_set, jnp.zeros((8, 128), f32))
    for owner in range(OWNERS):
        for j in range(4):
            head, tail = place_of(2 * owner + j // 2)
            lanes = slice(128 * (j % 2), 128 * (j % 2) + 128)
            answer[owner, 8 * j : 8 * j + 8, :] = total[head : head + 8, lanes]
            answer[owner, 32 + 4 * j : 36 + 4 * j, :] = total[tail : tail + 4, lanes]
        answer[owner, 48:56, :] = loss


def blend_scratch():
    return [
        pltpu.VMEM((768, 256), bf16),
        pltpu.VMEM((TOGETHER, ROWS, 128), bf16),
        pltpu.VMEM((TOGETHER, 48, ROWS), bf16),
        pltpu.VMEM((TOGETHER, ROWS, PIX), f32),
        pltpu.VMEM((TOGETHER, ROWS, PIX), f32),
        pltpu.VMEM((TOGETHER, ROWS, PIX), bf16),
        pltpu.VMEM((TOGETHER, ROWS, PIX), bf16),
        pltpu.VMEM((TOGETHER, 256, ROWS), bf16),
        pltpu.VMEM((TOGETHER, 16, ROWS), bf16),
        pltpu.VMEM((TOGETHER, ROWS, PIX), bf16),
        pltpu.VMEM((TOGETHER, 2, 16, ROWS), bf16),
        pltpu.VMEM((384, 256), f32),
    ]


def collect_kernel(back, wanted, aux, out, loss, total):
    total[...] = jnp.zeros_like(total)

    def one_band(band, squares):
        tops, lows, blocks, spots = [], [], [], []
        for j in range(4):
            value = jnp.concatenate(
                [
                    back[band, 8 * j : 8 * j + 8, :],
                    back[band, 32 + 4 * j : 36 + 4 * j, :],
                    jnp.zeros((4, 128), f32),
                ],
                axis=0,
            )
            high, low = halves(value)
            tops.append(high)
            lows.append(low)
            ids = jnp.broadcast_to(wanted[band, j : j + 1, :], (8, 128))
            blocks.append(lax.shift_right_logical(ids, 8))
            spots.append(ids & 255)
        high = jnp.concatenate(tops, axis=1)
        low = jnp.concatenate(lows, axis=1)
        block = jnp.concatenate(blocks, axis=1)
        spot = jnp.concatenate(spots, axis=1)
        left = masked_rows(small(block), 16, high, low)
        add_products(total, left, unit_rows(small(spot), CAP))
        return squares + back[band, 48:56, :]

    squares = lax.fori_loop(
        0, OWNERS, one_band, jnp.zeros((8, 128), f32), unroll=UNROLL_COLLECT
    )
    whole = jnp.sum(jnp.sum(squares, axis=1, keepdims=True), axis=0, keepdims=True)
    loss[...] = whole * (1.0 / (TILES * OWNERS * PIX * 3))
    for h in range(16):
        lanes = slice(256 * h, 256 * h + 256)
        head, tail = place_of(h)
        gain = [total[head + c : head + c + 1, :] for c in range(8)]
        gain += [total[tail + c : tail + c + 1, :] for c in range(4)]
        ca, sa, cb, sb, c0, c1, c2 = [aux[c : c + 1, lanes] for c in range(7)]
        cos_x, sin_x = 1.0 - 2.0 * sa * sa, 2.0 * sa * ca
        cos_y, sin_y = 1.0 - 2.0 * sb * sb, 2.0 * sb * cb
        d0 = (0.5 * KAPPA) * (cos_x * gain[1] + sin_x * gain[2] - gain[0])
        d2 = (0.5 * KAPPA) * (cos_y * gain[3] + sin_y * gain[4] - gain[0])
        cacb, casb, sacb, sasb = ca * cb, ca * sb, sa * cb, sa * sb
        d1 = (2.0 * KAPPA) * (casb * gain[6] - cacb * gain[5] + sacb * gain[7] - sasb * gain[8])
        twist = (2.0 * KAPPA) * c1
        da = KAPPA * c0 * (cos_x * gain[2] - sin_x * gain[1]) + twist * (
            sacb * gain[5] - sasb * gain[6] + cacb * gain[7] - casb * gain[8]
        )
        db = KAPPA * c2 * (cos_y * gain[4] - sin_y * gain[3]) + twist * (
            casb * gain[5] + cacb * gain[6] - sasb * gain[7] - sacb * gain[8]
        )
        out[0:1, lanes] = TURN * da
        out[1:2, lanes] = TURN * db
        out[2:3, lanes] = -(c0 * c0 * d0 + c0 * c1 * d1 + c1 * c1 * d2)
        out[3:4, lanes] = -(c0 * c1 * d0 + 0.5 * (c0 * c2 + c1 * c1) * d1 + c1 * c2 * d2)
        out[4:5, lanes] = -(c1 * c1 * d0 + c1 * c2 * d1 + c2 * c2 * d2)
        for c in range(3):
            raw = aux[7 + c : 8 + c, lanes]
            share = jnp.where(raw > 0.0, 1.0, jnp.where(raw == 0.0, 0.5, 0.0))
            out[5 + c : 6 + c, lanes] = share * gain[9 + c]
        spot = LOCAL + 256 * (h % 2)
        out[h // 2 : h // 2 + 1, spot : spot + 256] = gain[0]
    out[:, LOCAL + 512 :] = aux[0:8, LOCAL : LOCAL + 128]


def finish_kernel(
    near, far, log_scales, rotations, logit, grad_pos, grad_log, grad_rot, grad_op, grad_sh, work
):
    gathered = [ref.at[i] for ref in (near, far) for i in range(VIEWS // 2)]
    coef = jnp.concatenate([gathered[view][:, LOCAL + 512 :] for view in range(VIEWS)], axis=0)
    high, low = halves(coef.T)
    left = jnp.concatenate([high, low, high], axis=1)[0:64]
    for block in range(LOCAL // 512):
        lanes = slice(512 * block, 512 * block + 512)
        value = jnp.concatenate([gathered[view][:, lanes] for view in range(VIEWS)], axis=0)
        top, bottom = halves(value)
        right = jnp.concatenate([top, top, bottom], axis=0)
        work[:, lanes] = jnp.dot(left, right, preferred_element_type=f32)
    grad_sh[...] = work[0:48, :]
    grad_pos[...] = work[48:51, :]
    shade = gathered[0][:, LOCAL : LOCAL + 512]
    for view in range(1, VIEWS):
        shade = shade + gathered[view][:, LOCAL : LOCAL + 512]
    shade = jnp.concatenate([shade[s : s + 1, :] for s in range(8)], axis=1)
    grad_op[...] = shade / (1.0 + jnp.exp(logit[...]))
    k00, k01, k02, k11, k12, k22 = [work[51 + i : 52 + i, :] for i in range(6)]
    spread = [[k00, k01, k02], [k01, k11, k12], [k02, k12, k22]]
    inverse, (w, x, y, z), matrix = rotation([rotations[i : i + 1, :] for i in range(4)])
    d = [[None] * 3 for _ in range(3)]
    for j in range(3):
        scale = jnp.exp(log_scales[j : j + 1, :])
        square = scale * scale
        grad = None
        for i in range(3):
            value = (
                spread[i][0] * matrix[0][j]
                + spread[i][1] * matrix[1][j]
                + spread[i][2] * matrix[2][j]
            ) * square
            d[i][j] = value
            term = value * matrix[i][j]
            grad = term if grad is None else grad + term
        grad_log[j : j + 1, :] = grad
    dw = 2.0 * (x * (d[2][1] - d[1][2]) + y * (d[0][2] - d[2][0]) + z * (d[1][0] - d[0][1]))
    dx = 2.0 * (
        y * (d[0][1] + d[1][0])
        + z * (d[0][2] + d[2][0])
        + w * (d[2][1] - d[1][2])
        - 2.0 * x * (d[1][1] + d[2][2])
    )
    dy = 2.0 * (
        x * (d[0][1] + d[1][0])
        + z * (d[1][2] + d[2][1])
        + w * (d[0][2] - d[2][0])
        - 2.0 * y * (d[0][0] + d[2][2])
    )
    dz = 2.0 * (
        x * (d[0][2] + d[2][0])
        + y * (d[1][2] + d[2][1])
        + w * (d[1][0] - d[0][1])
        - 2.0 * z * (d[0][0] + d[1][1])
    )
    along = w * dw + x * dx + y * dy + z * dz
    for at, (part, unit) in enumerate(((dw, w), (dx, x), (dy, y), (dz, z))):
        grad_rot[at : at + 1, :] = (part - unit * along) * inverse


def whole():
    return pl.BlockSpec(memory_space=pltpu.VMEM)


def params(mega):
    return pltpu.CompilerParams(vmem_limit_bytes=mega << 20)


def shape(*dims):
    return jax.ShapeDtypeStruct(dims, f32)


def local(
    positions,
    log_scales,
    rotations,
    opacity_logit,
    sh_coeffs,
    view_angles,
    target,
    fetch_index,
    tile_slots,
    depth_order,
    block_count,
):
    wanted = lax.all_to_all(
        fetch_index.reshape(OWNERS, 4, 128), "band", split_axis=0, concat_axis=0, tiled=True
    )
    counts = jnp.tile(block_count.reshape(GROUPS, GROUP), (1, 16))
    front, back = pixel_tables()
    parts, aux = pl.pallas_call(
        project_kernel,
        out_shape=(jax.ShapeDtypeStruct((384, 256), bf16), shape(16, LOCAL + 128)),
        in_specs=[whole()] * 6,
        out_specs=(whole(), whole()),
        scratch_shapes=[pltpu.VMEM((16, LOCAL), f32)],
        compiler_params=params(24),
        name="project",
    )(view_angles, positions, log_scales, rotations, opacity_logit, sh_coeffs)
    send = pl.pallas_call(
        select_kernel,
        out_shape=shape(OWNERS, SEND_ROWS, 128),
        in_specs=[whole()] * 2,
        out_specs=whole(),
        compiler_params=params(32),
        name="select",
    )(wanted, parts)
    table = lax.all_to_all(send, "band", split_axis=0, concat_axis=0, tiled=True)
    images, answer = pl.pallas_call(
        blend_kernel,
        out_shape=(shape(TILES, 3, PIX), shape(OWNERS, BACK_ROWS, 128)),
        in_specs=[whole()] * 7,
        out_specs=(whole(), whole()),
        scratch_shapes=blend_scratch(),
        compiler_params=params(42),
        name="blend",
    )(
        table,
        tile_slots[0],
        depth_order[0],
        counts,
        target[0],
        jnp.asarray(front),
        jnp.asarray(back),
    )
    returned = lax.all_to_all(answer, "band", split_axis=0, concat_axis=0, tiled=True)
    share, loss = pl.pallas_call(
        collect_kernel,
        out_shape=(shape(8, WIDE), shape(1, 1)),
        in_specs=[whole()] * 3,
        out_specs=(whole(), whole()),
        scratch_shapes=[pltpu.VMEM((192, 256), f32)],
        compiler_params=params(32),
        name="collect",
    )(returned, wanted, aux)
    around = [share]
    for step in (4, 2, 6):
        ring = [(v, (v + step) % VIEWS) for v in range(VIEWS)]
        around.append(lax.ppermute(share, "view", ring))
    near = jnp.stack(around)
    far = lax.ppermute(near, "view", [(v, v ^ 1) for v in range(VIEWS)])
    grads = pl.pallas_call(
        finish_kernel,
        out_shape=(
            shape(3, LOCAL),
            shape(3, LOCAL),
            shape(4, LOCAL),
            shape(1, LOCAL),
            shape(48, LOCAL),
        ),
        in_specs=[whole()] * 5,
        out_specs=(whole(),) * 5,
        scratch_shapes=[pltpu.VMEM((64, LOCAL), f32)],
        compiler_params=params(32),
        name="finish",
    )(near, far, log_scales, rotations, opacity_logit)
    return (images[None], loss.reshape(1)) + tuple(grads)


def solution(mesh):
    in_specs = (
        P(None, "band"),
        P(None, "band"),
        P(None, "band"),
        P(None, "band"),
        P(None, "band"),
        P("view", None),
        P("view", "band", None, None),
        P("view", "band", None, None),
        P("view", "band", None),
        P("view", "band", None),
        P("view", "band"),
    )
    out_specs = (
        P("view", "band", None, None),
        P("view"),
        P(None, "band"),
        P(None, "band"),
        P(None, "band"),
        P(None, "band"),
        P(None, "band"),
    )
    return jax.shard_map(local, mesh=mesh, in_specs=in_specs, out_specs=out_specs, check_vma=False)
```

```python
import math

import jax
import jax.numpy as jnp
import ml_dtypes
import numpy as np
from jax import lax
from jax.experimental import pallas as pl
from jax.experimental.pallas import tpu as pltpu
from jax.sharding import PartitionSpec as P

SIDE = 16
PIX = SIDE * SIDE
SLOTS = 256
TILES = 48
CAP = 512
OWNERS = 16
LOCAL = 4096
VIEWS = 8
GROUP = 8
GROUPS = TILES // GROUP
ROWS = GROUP * SLOTS
CHUNK = 256
CHUNK_K = CHUNK // GROUP
CHUNKS = ROWS // CHUNK
SCAT = 512
BLOCK = 512
UNROLL_REDUCE = 4
TOGETHER = 3
UNROLL_GATHER = 4
UNROLL_FORWARD = 8
UNROLL_BACKWARD = 8
UNROLL_SCATTER = 4
UNROLL_SELECT = 8
UNROLL_COLLECT = 8
TURN = 2.0 * math.pi / SIDE
KAPPA = 0.5 / (TURN * TURN)
LOG2E = 1.4426950408889634
DEAD = -1024.0
SEND_ROWS = 48
BACK_ROWS = 56
WIDE = LOCAL + 512 + 128

f32 = jnp.float32
bf16 = jnp.bfloat16

zero_term = 0.28209479177387814
first_term = 0.4886025119029199
second_terms = (
    1.0925484305920792,
    -1.0925484305920792,
    0.31539156525252005,
    -1.0925484305920792,
    0.5462742152960396,
)
third_terms = (
    -0.5900435899266435,
    2.890611442640554,
    -0.4570457994644658,
    0.3731763325901154,
    -0.4570457994644658,
    1.445305721320277,
    -0.5900435899266435,
)
dilation = 0.3


def pixel_tables():
    pixel = np.arange(PIX)
    ang_x = TURN * (pixel % SIDE + 0.5)
    ang_y = TURN * (pixel // SIDE + 0.5)
    sx, cx, sy, cy = np.sin(ang_x), np.cos(ang_x), np.sin(ang_y), np.cos(ang_y)
    rows = np.stack(
        [
            np.ones(PIX),
            np.cos(2 * ang_x),
            np.sin(2 * ang_x),
            np.cos(2 * ang_y),
            np.sin(2 * ang_y),
            sx * sy,
            sx * cy,
            cx * sy,
            cx * cy,
        ]
    )
    kind = ml_dtypes.bfloat16
    parts = []
    rest = rows
    for _ in range(3):
        part = rest.astype(kind)
        parts.append(part)
        rest = rest - part.astype(np.float64)
    order = (0, 1, 2, 0, 1)
    front = np.zeros((128, PIX), kind)
    for at, which in enumerate(order):
        front[8 * at : 8 * at + 8] = parts[which][:8]
        front[40 + at] = parts[which][8]
    early = pixel % SIDE < SIDE // 2
    kept = np.where(np.arange(9)[:, None] < 5, early, ~early)
    back = np.zeros((32, PIX), kind)
    for at in (0, PIX // 2):
        half = slice(at, at + PIX // 2)
        back[0:9, half] = np.where(kept, parts[0], 0)[:, : PIX // 2]
        back[16:25, half] = np.where(kept, parts[1], 0)[:, : PIX // 2]
    return front, back


def harmonic_basis(dir_x, dir_y, dir_z):
    square_x = dir_x * dir_x
    square_y = dir_y * dir_y
    square_z = dir_z * dir_z
    return [
        zero_term + 0.0 * dir_x,
        -first_term * dir_y,
        first_term * dir_z,
        -first_term * dir_x,
        second_terms[0] * dir_x * dir_y,
        second_terms[1] * dir_y * dir_z,
        second_terms[2] * (2.0 * square_z - square_x - square_y),
        second_terms[3] * dir_x * dir_z,
        second_terms[4] * (square_x - square_y),
        third_terms[0] * dir_y * (3.0 * square_x - square_y),
        third_terms[1] * dir_x * dir_y * dir_z,
        third_terms[2] * dir_y * (4.0 * square_z - square_x - square_y),
        third_terms[3] * dir_z * (2.0 * square_z - 3.0 * square_x - 3.0 * square_y),
        third_terms[4] * dir_x * (4.0 * square_z - square_x - square_y),
        third_terms[5] * dir_z * (square_x - square_y),
        third_terms[6] * dir_x * (square_x - 3.0 * square_y),
    ]


def iota(shape, axis):
    return lax.broadcasted_iota(jnp.int32, shape, axis)


def wave(cycles):
    part = cycles - jnp.floor(cycles + 0.5)
    x = part * math.pi
    x2 = x * x
    sine = 1.0 / 6227020800.0
    for scale in (-1.0 / 39916800.0, 1.0 / 362880.0, -1.0 / 5040.0, 1.0 / 120.0, -1.0 / 6.0, 1.0):
        sine = sine * x2 + scale
    sine = sine * x
    cosine = -1.0 / 87178291200.0
    for scale in (
        1.0 / 479001600.0,
        -1.0 / 3628800.0,
        1.0 / 40320.0,
        -1.0 / 720.0,
        1.0 / 24.0,
        -0.5,
        1.0,
    ):
        cosine = cosine * x2 + scale
    return 2.0 * sine * cosine, 1.0 - 2.0 * sine * sine


def rotation(rows):
    length = jnp.sqrt(
        rows[0] * rows[0] + rows[1] * rows[1] + rows[2] * rows[2] + rows[3] * rows[3]
    )
    inverse = 1.0 / length
    w, x, y, z = [row * inverse for row in rows]
    matrix = [
        [1.0 - 2.0 * (y * y + z * z), 2.0 * (x * y - w * z), 2.0 * (x * z + w * y)],
        [2.0 * (x * y + w * z), 1.0 - 2.0 * (x * x + z * z), 2.0 * (y * z - w * x)],
        [2.0 * (x * z - w * y), 2.0 * (y * z + w * x), 1.0 - 2.0 * (x * x + y * y)],
    ]
    return inverse, (w, x, y, z), matrix


def halves(value):
    high = value.astype(bf16)
    low = (value - high.astype(f32)).astype(bf16)
    return high, low


def pick(table, lanes):
    return jnp.take_along_axis(table, lanes, axis=1)


def project_kernel(angles, positions, log_scales, rotations, logit, sh, parts, aux, tab):
    turns = 0.5 / math.pi
    sin_a, cos_a = wave(angles[0:1, 0:1] * turns)
    sin_e, cos_e = wave(angles[0:1, 1:2] * turns)
    right = (-sin_a, cos_a)
    upward = (-sin_e * cos_a, -sin_e * sin_a, cos_e)
    basis = harmonic_basis(cos_e * cos_a, cos_e * sin_a, sin_e)
    pos = [positions[i : i + 1, :] for i in range(3)]
    mean_x = right[0] * pos[0] + right[1] * pos[1]
    mean_y = upward[0] * pos[0] + upward[1] * pos[1] + upward[2] * pos[2]
    _, _, matrix = rotation([rotations[i : i + 1, :] for i in range(4)])
    scales = [jnp.exp(log_scales[i : i + 1, :]) for i in range(3)]
    first = [(right[0] * matrix[0][j] + right[1] * matrix[1][j]) * scales[j] for j in range(3)]
    second = [
        (upward[0] * matrix[0][j] + upward[1] * matrix[1][j] + upward[2] * matrix[2][j])
        * scales[j]
        for j in range(3)
    ]
    cov_a = first[0] * first[0] + first[1] * first[1] + first[2] * first[2] + dilation
    cov_b = first[0] * second[0] + first[1] * second[1] + first[2] * second[2]
    cov_c = second[0] * second[0] + second[1] * second[1] + second[2] * second[2] + dilation
    inverse = 1.0 / (cov_a * cov_c - cov_b * cov_b)
    c0, c1, c2 = cov_c * inverse, -cov_b * inverse, cov_a * inverse
    sa, ca = wave(mean_x * (1.0 / SIDE))
    sb, cb = wave(mean_y * (1.0 / SIDE))
    unit = KAPPA * LOG2E
    g0 = -LOG2E * jnp.log(1.0 + jnp.exp(-logit[...])) - (0.5 * unit) * (c0 + c2)
    cross = (-2.0 * unit) * c1
    half_x, half_y = (0.5 * unit) * c0, (0.5 * unit) * c2
    features = [
        g0,
        half_x * (1.0 - 2.0 * sa * sa),
        half_x * (2.0 * sa * ca),
        half_y * (1.0 - 2.0 * sb * sb),
        half_y * (2.0 * sb * cb),
        cross * ca * cb,
        -cross * ca * sb,
        -cross * sa * cb,
        cross * sa * sb,
    ]
    row48 = iota((48, 128), 0)
    weight = jnp.zeros((48, 128), f32)
    for k in range(16):
        weight = jnp.where(row48 // 3 == k, basis[k], weight)
    residue = row48 % 3
    masks = [jnp.where(residue == c, weight, 0.0) for c in range(3)]
    for block in range(LOCAL // 128):
        lanes = slice(128 * block, 128 * block + 128)
        piece = sh[:, lanes]
        for c in range(3):
            raw = 0.5 + jnp.sum(masks[c] * piece, axis=0, keepdims=True)
            aux[7 + c : 8 + c, lanes] = raw
            tab[9 + c : 10 + c, lanes] = jnp.maximum(raw, 0.0)
    for at, row in enumerate(features):
        tab[at : at + 1, :] = row
    for at, row in enumerate((ca, sa, cb, sb, c0, c1, c2)):
        aux[at : at + 1, 0:LOCAL] = row
    aux[10:16, 0:LOCAL] = jnp.zeros((6, LOCAL), f32)
    lane = iota((8, 128), 1)
    sub = iota((8, 128), 0)
    coef = jnp.zeros((8, 128), f32)
    for k in range(16):
        coef = jnp.where((lane // 3 == k) & (sub == 5 + lane % 3), basis[k], coef)

    def put(base, row, at, value):
        return jnp.where((sub == row) & (lane == at), value, base)

    for i in range(3):
        if i < 2:
            coef = put(coef, 0, 48 + i, right[i])
        coef = put(coef, 1, 48 + i, upward[i])
    at = 51
    for i in range(3):
        for j in range(i, 3):
            if j < 2:
                coef = put(coef, 2, at, 2.0 * right[i] * right[j])
            mixed = 0.0
            if i < 2:
                mixed = mixed + right[i] * upward[j]
            if j < 2:
                mixed = mixed + right[j] * upward[i]
            if i < 2 or j < 2:
                coef = put(coef, 3, at, 2.0 * mixed)
            coef = put(coef, 4, at, 2.0 * upward[i] * upward[j])
            at += 1
    aux[0:8, LOCAL : LOCAL + 128] = coef
    aux[8:16, LOCAL : LOCAL + 128] = jnp.zeros((8, 128), f32)

    for h in range(16):
        lanes = slice(256 * h, 256 * h + 256)
        value = tab[0:8, lanes]
        rest = tab[8:12, lanes]
        top = value.astype(bf16).astype(f32)
        peak = rest.astype(bf16).astype(f32)
        stack = jnp.concatenate([top, value - top, peak, rest - peak], axis=0)
        if h % 2 == 0:
            before = stack
        else:
            both = jnp.concatenate([before, stack], axis=0)
            parts[24 * h - 24 : 24 * h + 24, :] = both.astype(bf16)


def unit_rows(spot, width):
    row = iota((16, width), 0).astype(f32)
    one, zero = jnp.ones((16, width), bf16), jnp.zeros((16, width), bf16)
    return jnp.concatenate(
        [jnp.where(spot == (row + 16.0 * s).astype(bf16), one, zero) for s in range(16)], axis=0
    )


def small(ids):
    wide = ids.astype(f32)
    return jnp.concatenate([wide, wide], axis=0).astype(bf16)


def masked_rows(block, count, high, low):
    width = block.shape[1]
    row = iota((16, width), 0)
    by_eight = lax.shift_right_logical(row, 3).astype(f32)
    by_four = lax.shift_right_logical(row, 2).astype(f32)
    none = jnp.zeros((16, width), bf16)
    shares = []
    for value in (high, low):
        wide = value.astype(f32)
        head, tail = wide[0:8], wide[8:12]
        shares.append(
            (
                jnp.concatenate([head, head], axis=0).astype(bf16),
                jnp.concatenate([tail, tail, tail, tail], axis=0).astype(bf16),
            )
        )
    sets = ([], [])
    for h in range(0, count, 4):
        masks = [
            block == (by_eight + h).astype(bf16),
            block == (by_eight + (h + 2.0)).astype(bf16),
            block == (by_four + h).astype(bf16),
        ]
        for rows, (head, tail) in zip(sets, shares):
            rows.append(jnp.where(masks[0], head, none))
            rows.append(jnp.where(masks[1], head, none))
            rows.append(jnp.where(masks[2], tail, none))
    return jnp.concatenate(sets[0] + sets[1], axis=0)


def place_of(block):
    base = 48 * (block // 4)
    return base + 8 * (block % 4), base + 32 + 4 * (block % 4)


def add_products(total, left, hot):
    both = lax.dot_general(left, hot, (((1,), (1,)), ((), ())), preferred_element_type=f32)
    half = both.shape[0] // 2
    total[...] += both[0:half] + both[half:]


def select_kernel(wanted, parts, send):
    def one_band(band, carry):
        ids = jnp.concatenate(
            [jnp.broadcast_to(wanted[band, j : j + 1, :], (8, 128)) for j in range(4)], axis=1
        )
        block = lax.shift_right_logical(ids, 8)
        hot = unit_rows(small(ids & 255), CAP)
        found = jnp.dot(parts[...], hot, preferred_element_type=f32)
        acc = [jnp.zeros((8, CAP), f32)] * 3
        for h in range(16):
            mask = block == h
            for part in range(3):
                start = 24 * h + 8 * part
                acc[part] = jnp.where(mask, found[start : start + 8], acc[part])
        value = acc[0] + acc[1]
        rest = acc[2] + pltpu.roll(acc[2], 4, 0)
        for j in range(4):
            lanes = slice(128 * j, 128 * j + 128)
            send[band, 8 * j : 8 * j + 8, :] = value[:, lanes]
            send[band, 32 + 4 * j : 36 + 4 * j, :] = rest[0:4, lanes]
        return carry

    lax.fori_loop(0, OWNERS, one_band, 0, unroll=UNROLL_SELECT)


def blend_kernel(
    table,
    slots,
    order,
    counts,
    target,
    front,
    back,
    images,
    answer,
    tab,
    lhs,
    colours,
    alpha_ref,
    weight_ref,
    high_ref,
    low_ref,
    hot_ref,
    block_ref,
    fold_ref,
    grads,
    total,
):
    lane = iota((8, 128), 1)
    sub = iota((8, 128), 0)
    diagonal = sub == (lane & 7)
    diag_wide = iota((8, CHUNK), 0) == (iota((8, CHUNK), 1) & 7)
    depth = lax.shift_right_logical(lane, 3)
    early = (iota((CHUNK, 128), 1) & (SIDE - 1)) < SIDE // 2
    total[...] = jnp.zeros_like(total)
    for owner in range(OWNERS):
        pieces = []
        for part in range(2):
            tops, lows = [], []
            for j in (2 * part, 2 * part + 1):
                value = table[owner, 8 * j : 8 * j + 8, :]
                rest = table[owner, 32 + 4 * j : 36 + 4 * j, :]
                top = value.astype(bf16).astype(f32)
                peak = rest.astype(bf16).astype(f32)
                tops.append(jnp.concatenate([top, value - top, peak, rest - peak], axis=0))
            pieces.append(jnp.concatenate(tops, axis=1))
        tab[48 * owner : 48 * owner + 48, :] = jnp.concatenate(pieces, axis=0).astype(bf16)

    def one_set(index, loss):
        groups = [index * TOGETHER + g for g in range(TOGETHER)]
        starts = [pl.multiple_of(group * GROUP, GROUP) for group in groups]
        limits, ordered = [], []
        for g in range(TOGETHER):
            limits.append(jnp.broadcast_to(counts[pl.ds(groups[g], 1), :], (8, 128)))
            own = slots[pl.ds(starts[g], GROUP), :]
            sequence = order[pl.ds(starts[g], GROUP), :]
            for half in range(2):
                seq = sequence[:, 128 * half : 128 * half + 128]
                spot = seq & 127
                ordered.append(
                    jnp.where(seq < 128, pick(own[:, 0:128], spot), pick(own[:, 128:256], spot))
                )

        def gather(chunk, carry):
            at = pl.multiple_of(chunk * CHUNK, CHUNK)
            for g in range(TOGETHER):
                values = []
                for j in range(2):
                    base = (2 * chunk + j) * 16 + depth
                    value = jnp.where(
                        base < 128,
                        pick(ordered[2 * g], base & 127),
                        pick(ordered[2 * g + 1], base & 127),
                    )
                    value = jnp.sum(jnp.where(diagonal, value, 0), axis=0, keepdims=True)
                    values.append(jnp.broadcast_to(value, (8, 128)))
                ids = jnp.concatenate(values, axis=1)
                block = lax.shift_right_logical(ids, 8)
                hot = unit_rows(small(ids & 255), CHUNK)
                hot_ref[g, :, pl.ds(at, CHUNK)] = hot
                block_ref[g, :, pl.ds(at, CHUNK)] = small(block)
                found = jnp.dot(tab[...], hot, preferred_element_type=f32)
                acc = [jnp.zeros((8, CHUNK), f32)] * 3
                for h in range(32):
                    mask = block == h
                    for part in range(3):
                        start = 24 * h + 8 * part
                        acc[part] = jnp.where(mask, found[start : start + 8], acc[part])
                base = chunk * CHUNK_K + lax.shift_right_logical(iota((8, CHUNK), 1), 3)
                limit = jnp.concatenate([limits[g], limits[g]], axis=1)
                line = iota((8, CHUNK), 0)
                p1 = jnp.where((base >= limit) & (line == 0), DEAD, acc[0])
                p2 = acc[1]

                def spread(which):
                    return jnp.broadcast_to(acc[2][which : which + 1], (8, CHUNK))

                tail = jnp.where(line < 3, spread(0), jnp.where(line < 5, spread(4), 0.0))
                tops = [jnp.where(diag_wide, spread(1 + c), 0.0) for c in range(3)]
                lows = [jnp.where(diag_wide, spread(5 + c), 0.0) for c in range(3)]
                blank = jnp.zeros((8, CHUNK), f32)
                stack = jnp.concatenate(
                    [p1, p1, p1, p2, p2, tail, blank] + tops + tops + lows, axis=0
                )
                lhs[g, pl.ds(at, CHUNK), :] = stack.T.astype(bf16)
                colours[g, :, pl.ds(at, CHUNK)] = jnp.concatenate(tops + lows, axis=0).astype(bf16)
            return carry

        lax.fori_loop(0, CHUNKS, gather, 0, unroll=UNROLL_GATHER)

        def forward(chunk, carry):
            at = pl.multiple_of(chunk * CHUNK, CHUNK)
            result = []
            for g in range(TOGETHER):
                passing, picture = carry[2 * g], carry[2 * g + 1]
                power = jnp.dot(
                    lhs[g, pl.ds(at, CHUNK), :], front[...], preferred_element_type=f32
                )
                alpha = jnp.exp2(power)
                alpha_ref[g, pl.ds(at, CHUNK), :] = alpha
                pieces = []
                for k in range(CHUNK_K):
                    piece = alpha[8 * k : 8 * k + 8] * passing
                    passing = passing - piece
                    pieces.append(piece)
                weight = jnp.concatenate(pieces, axis=0)
                weight_ref[g, pl.ds(at, CHUNK), :] = weight
                high, low = halves(weight)
                high_ref[g, pl.ds(at, CHUNK), :] = high
                low_ref[g, pl.ds(at, CHUNK), :] = low
                own = colours[g, :, pl.ds(at, CHUNK)]
                picture = picture + jnp.dot(own, high, preferred_element_type=f32)
                picture = picture + jnp.dot(own, low, preferred_element_type=f32)
                result += [passing, picture]
            return tuple(result)

        begin = (jnp.ones((8, PIX), f32), jnp.zeros((48, PIX), f32)) * TOGETHER
        done = lax.fori_loop(0, CHUNKS, forward, begin, unroll=UNROLL_FORWARD)
        rights, errs = [], []
        for g in range(TOGETHER):
            picture = done[2 * g + 1]
            picture = picture[0:24] + picture[24:48]
            errors = []
            for c in range(3):
                image = picture[8 * c : 8 * c + 8]
                images[pl.ds(starts[g], GROUP), c, :] = image
                errors.append(image - target[pl.ds(starts[g], GROUP), c, :])
            for error in errors:
                square = error * error
                loss = loss + square[:, 0:128] + square[:, 128:256]
            error = jnp.concatenate(errors, axis=0)
            top = error.astype(bf16).astype(f32)
            bottom = error - top
            right = jnp.concatenate([jnp.zeros((56, PIX), f32), top, bottom, top], axis=0)
            rights.append(right.astype(bf16))
            errs.append(jnp.concatenate([top, bottom], axis=0))

        sides = []
        for g in range(TOGETHER):
            blank = jnp.zeros((96, PIX), f32)
            form = jnp.concatenate([back[...].astype(f32), blank], axis=0).T
            paint = jnp.concatenate([blank[0:32], errs[g], blank[0:48]], axis=0).T
            sides.append(jnp.concatenate([form, paint, paint], axis=0).astype(bf16))

        def backward(step, carry):
            at = pl.multiple_of((CHUNKS - 1 - step) * CHUNK, CHUNK)
            result = []
            for g in range(TOGETHER):
                behind = carry[g]
                gain = jnp.dot(
                    lhs[g, pl.ds(at, CHUNK), :], rights[g], preferred_element_type=f32
                )
                alpha = alpha_ref[g, pl.ds(at, CHUNK), :]
                weight = weight_ref[g, pl.ds(at, CHUNK), :]
                pieces = [None] * CHUNK_K
                for k in reversed(range(CHUNK_K)):
                    rows = slice(8 * k, 8 * k + 8)
                    gap = gain[rows] - behind
                    pieces[k] = weight[rows] * gap
                    behind = behind + alpha[rows] * gap
                result.append(behind)
                whole_rows = jnp.concatenate(pieces, axis=0)
                upper, lower = whole_rows[:, 0:128], whole_rows[:, 128:256]
                even, odd = upper + lower, upper - lower
                folded = jnp.where(
                    early, even + pltpu.roll(even, 120, 1), odd - pltpu.roll(odd, 8, 1)
                )
                fold_ref[g, pl.ds(at, CHUNK), :] = jnp.concatenate(halves(folded), axis=1)
            return tuple(result)

        lax.fori_loop(
            0,
            CHUNKS,
            backward,
            (jnp.zeros((8, PIX), f32),) * TOGETHER,
            unroll=UNROLL_BACKWARD,
        )

        def reduce(step, carry):
            at = pl.multiple_of(step * BLOCK, BLOCK)
            row = iota((8, BLOCK), 0)
            match = row == (iota((8, BLOCK), 1) & 7)
            for g in range(TOGETHER):
                pieces = [ref[g, pl.ds(at, BLOCK), :] for ref in (fold_ref, high_ref, low_ref)]
                sums = jnp.dot(
                    jnp.concatenate(pieces, axis=1), sides[g], preferred_element_type=f32
                ).T
                form = sums[0:16] + sums[16:32]
                paint = sums[32:56] + sums[56:80]
                second = form[8:16]
                for c in range(3):
                    own = jnp.where(match, paint[8 * c : 8 * c + 8], 0.0)
                    own = jnp.sum(own, axis=0, keepdims=True)
                    second = jnp.where(row == 1 + c, jnp.broadcast_to(own, (8, BLOCK)), second)
                high, low = halves(jnp.concatenate([form[0:8], second], axis=0))
                grads[g, 0, :, pl.ds(at, BLOCK)] = high
                grads[g, 1, :, pl.ds(at, BLOCK)] = low
            return carry

        lax.fori_loop(0, ROWS // BLOCK, reduce, 0, unroll=UNROLL_REDUCE)

        def scatter(step, carry):
            at = pl.multiple_of(step * SCAT, SCAT)
            for g in range(TOGETHER):
                block = block_ref[g, :, pl.ds(at, SCAT)]
                high = grads[g, 0, :, pl.ds(at, SCAT)]
                low = grads[g, 1, :, pl.ds(at, SCAT)]
                left = masked_rows(block, 32, high, low)
                add_products(total, left, hot_ref[g, :, pl.ds(at, SCAT)])
            return carry

        lax.fori_loop(0, ROWS // SCAT, scatter, 0, unroll=UNROLL_SCATTER)
        return loss

    loss = lax.fori_loop(0, GROUPS // TOGETHER, one_set, jnp.zeros((8, 128), f32))
    for owner in range(OWNERS):
        for j in range(4):
            head, tail = place_of(2 * owner + j // 2)
            lanes = slice(128 * (j % 2), 128 * (j % 2) + 128)
            answer[owner, 8 * j : 8 * j + 8, :] = total[head : head + 8, lanes]
            answer[owner, 32 + 4 * j : 36 + 4 * j, :] = total[tail : tail + 4, lanes]
        answer[owner, 48:56, :] = loss


def blend_scratch():
    return [
        pltpu.VMEM((768, 256), bf16),
        pltpu.VMEM((TOGETHER, ROWS, 128), bf16),
        pltpu.VMEM((TOGETHER, 48, ROWS), bf16),
        pltpu.VMEM((TOGETHER, ROWS, PIX), f32),
        pltpu.VMEM((TOGETHER, ROWS, PIX), f32),
        pltpu.VMEM((TOGETHER, ROWS, PIX), bf16),
        pltpu.VMEM((TOGETHER, ROWS, PIX), bf16),
        pltpu.VMEM((TOGETHER, 256, ROWS), bf16),
        pltpu.VMEM((TOGETHER, 16, ROWS), bf16),
        pltpu.VMEM((TOGETHER, ROWS, PIX), bf16),
        pltpu.VMEM((TOGETHER, 2, 16, ROWS), bf16),
        pltpu.VMEM((384, 256), f32),
    ]


def collect_kernel(back, wanted, aux, out, loss, total):
    total[...] = jnp.zeros_like(total)

    def one_band(band, squares):
        tops, lows, blocks, spots = [], [], [], []
        for j in range(4):
            value = jnp.concatenate(
                [
                    back[band, 8 * j : 8 * j + 8, :],
                    back[band, 32 + 4 * j : 36 + 4 * j, :],
                    jnp.zeros((4, 128), f32),
                ],
                axis=0,
            )
            high, low = halves(value)
            tops.append(high)
            lows.append(low)
            ids = jnp.broadcast_to(wanted[band, j : j + 1, :], (8, 128))
            blocks.append(lax.shift_right_logical(ids, 8))
            spots.append(ids & 255)
        high = jnp.concatenate(tops, axis=1)
        low = jnp.concatenate(lows, axis=1)
        block = jnp.concatenate(blocks, axis=1)
        spot = jnp.concatenate(spots, axis=1)
        left = masked_rows(small(block), 16, high, low)
        add_products(total, left, unit_rows(small(spot), CAP))
        return squares + back[band, 48:56, :]

    squares = lax.fori_loop(
        0, OWNERS, one_band, jnp.zeros((8, 128), f32), unroll=UNROLL_COLLECT
    )
    whole = jnp.sum(jnp.sum(squares, axis=1, keepdims=True), axis=0, keepdims=True)
    loss[...] = whole * (1.0 / (TILES * OWNERS * PIX * 3))
    for h in range(16):
        lanes = slice(256 * h, 256 * h + 256)
        head, tail = place_of(h)
        gain = [total[head + c : head + c + 1, :] for c in range(8)]
        gain += [total[tail + c : tail + c + 1, :] for c in range(4)]
        ca, sa, cb, sb, c0, c1, c2 = [aux[c : c + 1, lanes] for c in range(7)]
        cos_x, sin_x = 1.0 - 2.0 * sa * sa, 2.0 * sa * ca
        cos_y, sin_y = 1.0 - 2.0 * sb * sb, 2.0 * sb * cb
        d0 = (0.5 * KAPPA) * (cos_x * gain[1] + sin_x * gain[2] - gain[0])
        d2 = (0.5 * KAPPA) * (cos_y * gain[3] + sin_y * gain[4] - gain[0])
        cacb, casb, sacb, sasb = ca * cb, ca * sb, sa * cb, sa * sb
        d1 = (2.0 * KAPPA) * (casb * gain[6] - cacb * gain[5] + sacb * gain[7] - sasb * gain[8])
        twist = (2.0 * KAPPA) * c1
        da = KAPPA * c0 * (cos_x * gain[2] - sin_x * gain[1]) + twist * (
            sacb * gain[5] - sasb * gain[6] + cacb * gain[7] - casb * gain[8]
        )
        db = KAPPA * c2 * (cos_y * gain[4] - sin_y * gain[3]) + twist * (
            casb * gain[5] + cacb * gain[6] - sasb * gain[7] - sacb * gain[8]
        )
        out[0:1, lanes] = TURN * da
        out[1:2, lanes] = TURN * db
        out[2:3, lanes] = -(c0 * c0 * d0 + c0 * c1 * d1 + c1 * c1 * d2)
        out[3:4, lanes] = -(c0 * c1 * d0 + 0.5 * (c0 * c2 + c1 * c1) * d1 + c1 * c2 * d2)
        out[4:5, lanes] = -(c1 * c1 * d0 + c1 * c2 * d1 + c2 * c2 * d2)
        for c in range(3):
            raw = aux[7 + c : 8 + c, lanes]
            share = jnp.where(raw > 0.0, 1.0, jnp.where(raw == 0.0, 0.5, 0.0))
            out[5 + c : 6 + c, lanes] = share * gain[9 + c]
        spot = LOCAL + 256 * (h % 2)
        out[h // 2 : h // 2 + 1, spot : spot + 256] = gain[0]
    out[:, LOCAL + 512 :] = aux[0:8, LOCAL : LOCAL + 128]


def finish_kernel(
    near, far, log_scales, rotations, logit, grad_pos, grad_log, grad_rot, grad_op, grad_sh, work
):
    gathered = [ref.at[i] for ref in (near, far) for i in range(VIEWS // 2)]
    coef = jnp.concatenate([gathered[view][:, LOCAL + 512 :] for view in range(VIEWS)], axis=0)
    high, low = halves(coef.T)
    left = jnp.concatenate([high, low, high], axis=1)[0:64]
    for block in range(LOCAL // 512):
        lanes = slice(512 * block, 512 * block + 512)
        value = jnp.concatenate([gathered[view][:, lanes] for view in range(VIEWS)], axis=0)
        top, bottom = halves(value)
        right = jnp.concatenate([top, top, bottom], axis=0)
        work[:, lanes] = jnp.dot(left, right, preferred_element_type=f32)
    grad_sh[...] = work[0:48, :]
    grad_pos[...] = work[48:51, :]
    shade = gathered[0][:, LOCAL : LOCAL + 512]
    for view in range(1, VIEWS):
        shade = shade + gathered[view][:, LOCAL : LOCAL + 512]
    shade = jnp.concatenate([shade[s : s + 1, :] for s in range(8)], axis=1)
    grad_op[...] = shade / (1.0 + jnp.exp(logit[...]))
    k00, k01, k02, k11, k12, k22 = [work[51 + i : 52 + i, :] for i in range(6)]
    spread = [[k00, k01, k02], [k01, k11, k12], [k02, k12, k22]]
    inverse, (w, x, y, z), matrix = rotation([rotations[i : i + 1, :] for i in range(4)])
    d = [[None] * 3 for _ in range(3)]
    for j in range(3):
        scale = jnp.exp(log_scales[j : j + 1, :])
        square = scale * scale
        grad = None
        for i in range(3):
            value = (
                spread[i][0] * matrix[0][j]
                + spread[i][1] * matrix[1][j]
                + spread[i][2] * matrix[2][j]
            ) * square
            d[i][j] = value
            term = value * matrix[i][j]
            grad = term if grad is None else grad + term
        grad_log[j : j + 1, :] = grad
    dw = 2.0 * (x * (d[2][1] - d[1][2]) + y * (d[0][2] - d[2][0]) + z * (d[1][0] - d[0][1]))
    dx = 2.0 * (
        y * (d[0][1] + d[1][0])
        + z * (d[0][2] + d[2][0])
        + w * (d[2][1] - d[1][2])
        - 2.0 * x * (d[1][1] + d[2][2])
    )
    dy = 2.0 * (
        x * (d[0][1] + d[1][0])
        + z * (d[1][2] + d[2][1])
        + w * (d[0][2] - d[2][0])
        - 2.0 * y * (d[0][0] + d[2][2])
    )
    dz = 2.0 * (
        x * (d[0][2] + d[2][0])
        + y * (d[1][2] + d[2][1])
        + w * (d[1][0] - d[0][1])
        - 2.0 * z * (d[0][0] + d[1][1])
    )
    along = w * dw + x * dx + y * dy + z * dz
    for at, (part, unit) in enumerate(((dw, w), (dx, x), (dy, y), (dz, z))):
        grad_rot[at : at + 1, :] = (part - unit * along) * inverse


def whole():
    return pl.BlockSpec(memory_space=pltpu.VMEM)


def params(mega):
    return pltpu.CompilerParams(vmem_limit_bytes=mega << 20)


def shape(*dims):
    return jax.ShapeDtypeStruct(dims, f32)


def local(
    positions,
    log_scales,
    rotations,
    opacity_logit,
    sh_coeffs,
    view_angles,
    target,
    fetch_index,
    tile_slots,
    depth_order,
    block_count,
):
    wanted = lax.all_to_all(
        fetch_index.reshape(OWNERS, 4, 128), "band", split_axis=0, concat_axis=0, tiled=True
    )
    counts = jnp.tile(block_count.reshape(GROUPS, GROUP), (1, 16))
    front, back = pixel_tables()
    parts, aux = pl.pallas_call(
        project_kernel,
        out_shape=(jax.ShapeDtypeStruct((384, 256), bf16), shape(16, LOCAL + 128)),
        in_specs=[whole()] * 6,
        out_specs=(whole(), whole()),
        scratch_shapes=[pltpu.VMEM((16, LOCAL), f32)],
        compiler_params=params(24),
        name="project",
    )(view_angles, positions, log_scales, rotations, opacity_logit, sh_coeffs)
    send = pl.pallas_call(
        select_kernel,
        out_shape=shape(OWNERS, SEND_ROWS, 128),
        in_specs=[whole()] * 2,
        out_specs=whole(),
        compiler_params=params(32),
        name="select",
    )(wanted, parts)
    table = lax.all_to_all(send, "band", split_axis=0, concat_axis=0, tiled=True)
    images, answer = pl.pallas_call(
        blend_kernel,
        out_shape=(shape(TILES, 3, PIX), shape(OWNERS, BACK_ROWS, 128)),
        in_specs=[whole()] * 7,
        out_specs=(whole(), whole()),
        scratch_shapes=blend_scratch(),
        compiler_params=params(42),
        name="blend",
    )(
        table,
        tile_slots[0],
        depth_order[0],
        counts,
        target[0],
        jnp.asarray(front),
        jnp.asarray(back),
    )
    returned = lax.all_to_all(answer, "band", split_axis=0, concat_axis=0, tiled=True)
    share, loss = pl.pallas_call(
        collect_kernel,
        out_shape=(shape(8, WIDE), shape(1, 1)),
        in_specs=[whole()] * 3,
        out_specs=(whole(), whole()),
        scratch_shapes=[pltpu.VMEM((192, 256), f32)],
        compiler_params=params(32),
        name="collect",
    )(returned, wanted, aux)
    around = [share]
    for step in (2, 6, 4):
        ring = [(v, (v + step) % VIEWS) for v in range(VIEWS)]
        around.append(lax.ppermute(share, "view", ring))
    near = jnp.stack(around)
    far = lax.ppermute(near, "view", [(v, v ^ 1) for v in range(VIEWS)])
    grads = pl.pallas_call(
        finish_kernel,
        out_shape=(
            shape(3, LOCAL),
            shape(3, LOCAL),
            shape(4, LOCAL),
            shape(1, LOCAL),
            shape(48, LOCAL),
        ),
        in_specs=[whole()] * 5,
        out_specs=(whole(),) * 5,
        scratch_shapes=[pltpu.VMEM((64, LOCAL), f32)],
        compiler_params=params(32),
        name="finish",
    )(near, far, log_scales, rotations, opacity_logit)
    return (images[None], loss.reshape(1)) + tuple(grads)


def solution(mesh):
    in_specs = (
        P(None, "band"),
        P(None, "band"),
        P(None, "band"),
        P(None, "band"),
        P(None, "band"),
        P("view", None),
        P("view", "band", None, None),
        P("view", "band", None, None),
        P("view", "band", None),
        P("view", "band", None),
        P("view", "band"),
    )
    out_specs = (
        P("view", "band", None, None),
        P("view"),
        P(None, "band"),
        P(None, "band"),
        P(None, "band"),
        P(None, "band"),
        P(None, "band"),
    )
    return jax.shard_map(local, mesh=mesh, in_specs=in_specs, out_specs=out_specs, check_vma=False)
```
